32 devices in a mesh: seq: 16 (over z, y, x), tp: 2 (over core).
Axes of the slice: x: 2, y: 2, z: 4, core: 2. Of those that a mesh axis runs over, the one named last changes fastest.
Arguments:
- tokens: bfloat16 [128, 16, 2048], P('seq', None, 'tp'), may hold values from -6 to 6
- gain_in: bfloat16 [2048], replicated, may hold values from 0.25 to 1.75
- w_qkv: bfloat16 [3, 2048, 2048], P(None, None, 'tp'), may hold values from -0.125 to 0.125
- w_beta: bfloat16 [2048, 16], P(None, 'tp'), may hold values from -0.25 to 0.25
- conv_weight: bfloat16 [4, 3, 2048], P(None, None, 'tp'), may hold values from -3 to 3
- out_gain: bfloat16 [128], replicated, may hold values from 0.25 to 1.75
- w_out: bfloat16 [2048, 2048], P('tp'), may hold values from -0.125 to 0.125
- state_pages: bfloat16 [128, 16, 128, 128], P('seq', 'tp'), may hold values from -4 to 4
- conv_pages: bfloat16 [128, 3, 3, 2048], P('seq', None, None, 'tp'), may hold values from -6 to 6
- page_order: int32 [128], replicated, may hold values from 0 to 127, as said below
- draft_lengths: int32 [128], replicated, may hold values from 1 to 16
- accepted: int32 [128], replicated, may hold values from 0 to 16
Outputs:
- mixed: bfloat16 [128, 16, 2048], P('seq', None, 'tp')
- final_pages: bfloat16 [128, 16, 128, 128], P('seq', 'tp')
- final_conv: bfloat16 [128, 3, 3, 2048], P('seq', None, None, 'tp')
The draws below stay inside these ranges and needn't reach their ends.
Inputs may be any that keep to these rules, and one draw needn't show every extreme that they name: page_order is a permutation of all requests; slot s lies on seq device s // 8 and holds a request r of the same device (r // 8) or of one of the two devices next to it along seq, taken cyclically; the slots of one device that hold requests of one neighbour are at most 4, exactly 4 for some pair of devices, and as many as the slots of that neighbour that hold requests of the first device.
All inputs are finite; a program needn't handle non-finite values.
Results may differ from the reference program's by a relative error of at most 0.015.
Values may be sent and summed in bfloat16 or wider, within the bound.
A program may use at most 64 MiB of HBM per device.

```python
import jax
import jax.numpy as jnp
from jax import lax

D = 2048
HEADS = 16
DK = 128
CONV = 4
DRAFT = 16
REQUESTS_PER_SEQ = 8
MOVE = 4
REQS = 128
N_SEQ = 16
N_TP = 2


def draw_page_order(key, part):
    devices = REQS // REQUESTS_PER_SEQ
    key_counts, key_where, key_labels, key_slots = jax.random.split(key, 4)
    counts = jax.random.randint(key_counts, (devices,), 0, MOVE + 1).astype(jnp.int32)
    fullest = jax.random.randint(key_where, (), 0, devices).astype(jnp.int32)
    counts = jnp.where(jnp.arange(devices, dtype=jnp.int32) == fullest, MOVE, counts).astype(jnp.int32)
    lower = jnp.roll(counts, 1)[:, None]
    upper = REQUESTS_PER_SEQ - counts[:, None]
    device_ids = jnp.arange(devices, dtype=jnp.int32)[:, None]
    local = jnp.arange(REQUESTS_PER_SEQ, dtype=jnp.int32)[None, :]
    from_before = (device_ids + devices - 1) % devices * REQUESTS_PER_SEQ + REQUESTS_PER_SEQ - lower + local
    own_rows = device_ids * REQUESTS_PER_SEQ + local
    from_after = (device_ids + 1) % devices * REQUESTS_PER_SEQ + local - upper
    standard_labels = jnp.where(local < lower, from_before, jnp.where(local < upper, own_rows, from_after)).astype(jnp.int32)
    label_values = jax.vmap(lambda one_key: jax.random.permutation(one_key, REQUESTS_PER_SEQ))(jax.random.split(key_labels, devices)).astype(jnp.int32)
    owning_device = standard_labels // REQUESTS_PER_SEQ
    renamed_labels = owning_device * REQUESTS_PER_SEQ + label_values[owning_device, standard_labels % REQUESTS_PER_SEQ]
    random_orders = jax.vmap(lambda one_key: jax.random.permutation(one_key, REQUESTS_PER_SEQ))(jax.random.split(key_slots, devices)).astype(jnp.int32)
    final_result = jnp.take_along_axis(renamed_labels, random_orders, axis=1)
    return final_result.reshape(-1).astype(jnp.int32)


def set_ends(entries, own_key, low, high):
    extent = entries.shape
    spot = [jax.random.randint(jax.random.fold_in(own_key, axis), (), 0, extent[axis]) for axis in range(len(extent))]
    entries = entries.at[tuple(spot)].set(low)
    longest = extent.index(max(extent))
    spot[longest] = (spot[longest] + 1) % extent[longest]
    return entries.at[tuple(spot)].set(high)


def level_of(rng, shape, pieces, smallest, largest):
    loudness = 1.0
    for position, blocks in pieces:
        steps = jax.random.uniform(jax.random.fold_in(jax.random.fold_in(rng, 6), position), (blocks,), jnp.float32, smallest / len(pieces), largest / len(pieces))
        loudness = loudness * jnp.repeat(jnp.exp(steps), shape[position] // blocks).reshape((-1,) + (1,) * (len(shape) - 1 - position))
    return loudness


def centred(stream_key, dims, spread, most, shards=(), held_as=jnp.bfloat16):
    array = spread * jax.random.normal(stream_key, dims, jnp.float32)
    if shards:
        array = array * level_of(stream_key, dims, shards, -0.22, 0.18)
    return jnp.clip(array, -most, most).astype(held_as)


def setup_inputs(seed: int = 0) -> dict:
    splits = jax.random.split(jax.random.key(seed), 13)
    tokens = centred(splits[0], (REQS, DRAFT, D), 1.0, 6.0, ((0, 16), (2, 2)))
    gain_in = jnp.clip(1.0 + 0.15 * jax.random.normal(splits[1], (D,), jnp.float32), 0.25, 1.75).astype(jnp.bfloat16)
    w_qkv = centred(splits[2], (3, D, HEADS * DK), D ** -0.5, 0.125, ((2, 2),))
    w_beta = centred(splits[3], (D, HEADS), (D // 4) ** -0.5, 0.25, ((1, 2),))
    conv_weight = centred(splits[4], (CONV, 3, HEADS * DK), 0.6, 3.0, ((2, 2),))
    out_gain = jnp.clip(1.0 + 0.15 * jax.random.normal(splits[5], (DK,), jnp.float32), 0.25, 1.75).astype(jnp.bfloat16)
    w_out = centred(splits[6], (HEADS * DK, D), (HEADS * DK) ** -0.5, 0.125, ((0, 2),))
    state_pages = centred(splits[7], (REQS, HEADS, DK, DK), 0.5, 4.0, ((0, 16), (1, 2)))
    conv_pages = centred(splits[8], (REQS, CONV - 1, 3, HEADS * DK), 1.0, 6.0, ((0, 16), (3, 2)))
    page_order = draw_page_order(jax.random.fold_in(splits[12], 71), 0)
    draft_lengths = set_ends(jax.random.randint(splits[10], (REQS,), 1, DRAFT + 1), jax.random.fold_in(splits[10], 1), 1, DRAFT).astype(jnp.int32)
    accepted = set_ends(jax.random.randint(splits[11], (REQS,), 0, DRAFT + 1), jax.random.fold_in(splits[11], 1), 0, DRAFT).astype(jnp.int32)
    return dict(tokens=tokens, gain_in=gain_in, w_qkv=w_qkv, w_beta=w_beta, conv_weight=conv_weight, out_gain=out_gain, w_out=w_out, state_pages=state_pages, conv_pages=conv_pages, page_order=page_order, draft_lengths=draft_lengths, accepted=accepted)


def rms_rows(values, gain):
    wide = values.astype(jnp.float32)
    return wide * lax.rsqrt(lax.optimization_barrier(jnp.mean(wide * wide, axis=-1, keepdims=True)) + 1e-06) * gain.astype(jnp.float32)

def unit_heads(values):
    return values * lax.rsqrt(lax.optimization_barrier(jnp.sum(values * values, axis=-1, keepdims=True)) + 1e-06)

def reference(tokens, gain_in, w_qkv, w_beta, conv_weight, out_gain, w_out, state_pages, conv_pages, page_order, draft_lengths, accepted):
    hidden_dim = HEADS * DK
    group_width = hidden_dim // N_TP
    inverse = jnp.zeros((REQS,), jnp.int32).at[page_order].set(jnp.arange(REQS, dtype=jnp.int32))

    def per_block(packed):
        block, lengths, counts, pages, caches = packed
        normed = rms_rows(block, gain_in).astype(jnp.bfloat16)
        projected = jnp.einsum('rtd,cde->rtce', normed.astype(jnp.float32), w_qkv.astype(jnp.float32)).astype(jnp.bfloat16)
        extended = jnp.concatenate([caches, projected], axis=1)
        summed = jnp.zeros(projected.shape, jnp.float32)
        for offset in range(CONV):
            summed = summed + extended[:, offset:offset + DRAFT].astype(jnp.float32) * conv_weight[offset].astype(jnp.float32)
        active = jax.nn.silu(summed).reshape(REQUESTS_PER_SEQ, DRAFT, 3, HEADS, DK)
        queries = jnp.moveaxis(unit_heads(active[:, :, 0]) * DK ** (-0.5), 1, 0)
        keys_all = jnp.moveaxis(unit_heads(active[:, :, 1]), 1, 0)
        values_all = jnp.moveaxis(active[:, :, 2], 1, 0)
        live = jnp.arange(DRAFT, dtype=jnp.int32)[None, :] < lengths[:, None]
        rates = jax.nn.sigmoid(jnp.dot(normed.reshape(-1, D), w_beta, preferred_element_type=jnp.float32)).reshape(REQUESTS_PER_SEQ, DRAFT, HEADS)
        rates = jnp.moveaxis(rates * live[:, :, None].astype(jnp.float32), 1, 0)
        kept = jnp.minimum(counts, lengths)
        start = pages.astype(jnp.float32)

        def advance(carry, inputs):
            state, snapshot = carry
            query, key_t, value, rate, index = inputs
            recalled = jnp.einsum('rhkv,rhk->rhv', state, key_t, precision=lax.Precision.HIGHEST)
            state = state + (rate[..., None] * key_t)[..., :, None] * (value - recalled)[..., None, :]
            output = jnp.einsum('rhkv,rhk->rhv', state, query, precision=lax.Precision.HIGHEST)
            snapshot = jnp.where((kept == index + 1)[:, None, None, None], state, snapshot)
            return ((state, snapshot), output)
        steps_in = (queries, keys_all, values_all, rates, jnp.arange(DRAFT, dtype=jnp.int32))
        (last_state, snapshot), outputs = lax.scan(advance, (start, start), steps_in)
        normed_out = rms_rows(jnp.moveaxis(outputs, 0, 1), out_gain).astype(jnp.bfloat16).reshape(REQUESTS_PER_SEQ * DRAFT, hidden_dim)
        attended = jnp.zeros((REQUESTS_PER_SEQ * DRAFT, D), jnp.float32)
        for group in range(N_TP):
            lo_col = group * group_width
            part_sum = jnp.dot(normed_out[:, lo_col:lo_col + group_width], w_out[lo_col:lo_col + group_width], preferred_element_type=jnp.float32)
            attended = attended + part_sum.astype(jnp.bfloat16).astype(jnp.float32)
        mixed = (block.reshape(-1, D).astype(jnp.float32) + attended).astype(jnp.bfloat16).reshape(REQUESTS_PER_SEQ, DRAFT, D)
        mixed = jnp.where(live[:, :, None], mixed, jnp.zeros_like(mixed))
        picks = kept[:, None] + jnp.arange(CONV - 1, dtype=jnp.int32)[None, :]
        edges = jnp.take_along_axis(extended, picks[:, :, None, None], axis=1)
        return (mixed, snapshot.astype(jnp.bfloat16), edges)
    packed = (tokens.reshape(N_SEQ, REQUESTS_PER_SEQ, DRAFT, D), draft_lengths.reshape(N_SEQ, REQUESTS_PER_SEQ), accepted.reshape(N_SEQ, REQUESTS_PER_SEQ), jnp.take(state_pages, inverse, axis=0).reshape(N_SEQ, REQUESTS_PER_SEQ, HEADS, DK, DK), jnp.take(conv_pages, inverse, axis=0).reshape(N_SEQ, REQUESTS_PER_SEQ, CONV - 1, 3, hidden_dim))
    mixed, by_request, edges_out = lax.map(per_block, packed)
    return (mixed.reshape(REQS, DRAFT, D), jnp.take(by_request.reshape(REQS, HEADS, DK, DK), page_order, axis=0), jnp.take(edges_out.reshape(REQS, CONV - 1, 3, hidden_dim), page_order, axis=0))
```

```python
import functools

import jax
import jax.numpy as jnp
from jax import lax
from jax.experimental import pallas as pl
from jax.experimental.pallas import tpu as pltpu
from jax.sharding import PartitionSpec as P

DK = 128
CONV = 4
MOVE = 4
HIST = CONV - 1
EXT0 = 8 - HIST
F32 = jnp.float32
BF16 = jnp.bfloat16
MESH = pl.DeviceIdType.MESH


def split(wide):
    high = wide.astype(BF16)
    return high, (wide - high.astype(F32)).astype(BF16)


def unit(values):
    return values * lax.rsqrt(jnp.sum(values * values, axis=-1, keepdims=True) + 1e-06)


def matches(po_ref, device, home, reqs):
    found = []
    count = jnp.int32(0)
    for j in range(reqs):
        request = po_ref[device * reqs + j]
        hit = (request >= home * reqs) & (request < home * reqs + reqs)
        found.append((request, hit, count))
        count = count + hit.astype(jnp.int32)
    return found


def pick_rank(found, rank, values):
    total = jnp.int32(0)
    for (_, hit, place), value in zip(found, values):
        total = total + jnp.where(hit & (place == rank), value, 0)
    return jnp.clip(total, 0, len(values) - 1)


def kernel(
    n_seq,
    n_tp,
    po_ref,
    len_ref,
    acc_ref,
    tok_ref,
    gain_ref,
    wb_ref,
    cw_ref,
    og_ref,
    conv_ref,
    wqkv_hbm,
    wout_hbm,
    state_hbm,
    mixed_ref,
    fconv_ref,
    pages_hbm,
    wq,
    wo,
    st,
    pool,
    send_l,
    send_r,
    xs,
    normed,
    ext,
    beta,
    on,
    kc,
    uc,
    part,
    part_in,
    done,
    back,
    back_l,
    back_r,
    w_sem,
    wo_sem,
    st_sem,
    out_sem,
    mig_send,
    mig_recv,
    tp_send,
    tp_recv,
    rs_send,
    rs_recv,
    ret_send,
    ret_recv,
):
    reqs, drafts, cols = tok_ref.shape
    rows = reqs * drafts
    heads = state_hbm.shape[1]
    hidden = heads * DK
    group = 2 if heads % 2 == 0 else 1
    width = group * DK
    tiles = heads // group
    me = lax.axis_index("seq")
    mt = lax.axis_index("tp")
    left = lax.rem(me + n_seq - 1, n_seq)
    right = lax.rem(me + 1, n_seq)

    def w_copy(i):
        at = pl.ds(pl.multiple_of(i * width, width), width)
        return pltpu.make_async_copy(wqkv_hbm.at[:, :, at], wq.at[:, :, at], w_sem.at[i])

    st_copy = pltpu.make_async_copy(state_hbm, st, st_sem)
    wo_copy = pltpu.make_async_copy(wout_hbm, wo, wo_sem)
    w_copy(0).start()
    st_copy.start()
    for i in range(1, tiles):
        w_copy(i).start()
    wo_copy.start()

    barrier = pltpu.get_barrier_semaphore()
    for other in (left, right):
        pl.semaphore_signal(barrier, inc=1, device_id={"seq": other}, device_id_type=MESH)
    for j in range(1, n_tp):
        pl.semaphore_signal(
            barrier, inc=1, device_id={"tp": lax.rem(mt + j, n_tp)}, device_id_type=MESH
        )

    own = matches(po_ref, me, me, reqs)
    from_l = matches(po_ref, me, left, reqs)
    from_r = matches(po_ref, me, right, reqs)
    at_l = matches(po_ref, left, me, reqs)
    at_r = matches(po_ref, right, me, reqs)
    base = me * reqs
    for k in range(MOVE):
        send_l[k] = tok_ref[pick_rank(at_l, k, [f[0] - base for f in at_l])]
        send_r[k] = tok_ref[pick_rank(at_r, k, [f[0] - base for f in at_r])]
    pl.semaphore_wait(barrier, 2 + n_tp - 1)

    def exchange(src_l, src_r, dst, send_sem, recv_sem):
        to_r = pltpu.make_async_remote_copy(
            src_ref=src_r,
            dst_ref=dst.at[pl.ds(reqs, MOVE)],
            send_sem=send_sem.at[0],
            recv_sem=recv_sem.at[0],
            device_id={"seq": right},
            device_id_type=MESH,
        )
        to_l = pltpu.make_async_remote_copy(
            src_ref=src_l,
            dst_ref=dst.at[pl.ds(reqs + MOVE, MOVE)],
            send_sem=send_sem.at[1],
            recv_sem=recv_sem.at[1],
            device_id={"seq": left},
            device_id_type=MESH,
        )
        to_r.start()
        to_l.start()
        return to_r, to_l

    moves = exchange(send_l, send_r, pool.at[mt], mig_send, mig_recv)

    def to_peers(src, dst, stage):
        copies = []
        for j in range(1, n_tp):
            copy = pltpu.make_async_remote_copy(
                src_ref=src,
                dst_ref=dst,
                send_sem=tp_send.at[stage, j],
                recv_sem=tp_recv.at[stage, j],
                device_id={"tp": lax.rem(mt + j, n_tp)},
                device_id_type=MESH,
            )
            copy.start()
            copies.append(copy)
        return copies

    gathers = to_peers(tok_ref, pool.at[mt, pl.ds(0, reqs)], 0)
    pool[mt, pl.ds(0, reqs)] = tok_ref[...]

    lengths = []
    keeps = []
    places = []
    for j in range(reqs):
        request, hit, _ = own[j]
        lengths.append(len_ref[request])
        keeps.append(jnp.minimum(acc_ref[request], lengths[j]))
        place = jnp.where(from_l[j][1], reqs + from_l[j][2], reqs + MOVE + from_r[j][2])
        place = jnp.where(hit, request - base, place)
        places.append(jnp.clip(place, 0, reqs + 2 * MOVE - 1))
    homes = []
    for i in range(reqs):
        place = jnp.int32(0)
        for j in range(reqs):
            place = jnp.where(own[j][0] == base + i, j, place)
            place = jnp.where(at_l[j][0] == base + i, reqs + at_l[j][2], place)
            place = jnp.where(at_r[j][0] == base + i, reqs + MOVE + at_r[j][2], place)
        homes.append(jnp.clip(place, 0, reqs + 2 * MOVE - 1))
    slots = list(range(reqs))
    back_to_l = [pick_rank(from_l, k, slots) for k in range(MOVE)]
    back_to_r = [pick_rank(from_r, k, slots) for k in range(MOVE)]
    req_of = lax.broadcasted_iota(jnp.int32, (reqs, drafts, 1), 0)
    step_of = lax.broadcasted_iota(jnp.int32, (reqs, drafts, 1), 1)
    live = jnp.zeros((reqs, drafts, 1), jnp.int32)
    kept = jnp.zeros((reqs, drafts, 1), jnp.int32)
    for j in range(reqs):
        live = jnp.where(req_of == j, lengths[j], live)
        kept = jnp.where(req_of == j, keeps[j], kept)
    live = (step_of < live).astype(F32)
    kept = (step_of < kept).astype(F32)
    for e in range(HIST):
        for c in range(3):
            ext[c, :, EXT0 + e, :] = conv_ref[e, c].astype(F32)

    for copy in moves:
        copy.wait()
    gathers += to_peers(
        pool.at[mt, pl.ds(reqs, 2 * MOVE)], pool.at[mt, pl.ds(reqs, 2 * MOVE)], 1
    )
    for copy in gathers:
        copy.wait()

    gain = gain_ref[...].astype(F32)
    for j in range(reqs):
        for c in range(n_tp):
            xs[j, :, pl.ds(c * cols, cols)] = pool[c, places[j]]
        wide = xs[j].astype(F32)
        scale = lax.rsqrt(jnp.mean(wide * wide, axis=-1, keepdims=True) + 1e-06)
        normed[pl.ds(j * drafts, drafts), :] = (wide * scale * gain).astype(BF16)
    rates = jax.nn.sigmoid(
        lax.dot_general(
            normed[...], wb_ref[...], (((1,), (1,)), ((), ())), preferred_element_type=F32
        )
    )
    beta[...] = rates * live.reshape(rows, 1)

    st_copy.wait()
    row_of = lax.broadcasted_iota(jnp.int32, (rows, rows), 0)
    col_of = lax.broadcasted_iota(jnp.int32, (rows, rows), 1)
    causal = (row_of // drafts == col_of // drafts) & (col_of <= row_of)
    half = drafts // 2
    t_half = lax.broadcasted_iota(jnp.int32, (1, half, 1), 1)
    head_of = lax.broadcasted_iota(jnp.int32, (rows, heads), 1)
    out_gain = og_ref[...].astype(F32)

    def tile(i, _):
        at = pl.ds(pl.multiple_of(i * width, width), width)
        w_copy(i).wait()
        acts = []
        for c in range(3):
            proj = jnp.dot(normed[...], wq[c, :, at], preferred_element_type=F32)
            ext[c, :, pl.ds(8, drafts), at] = (
                proj.astype(BF16).astype(F32).reshape(reqs, drafts, width)
            )
            taps = cw_ref[c, :, at].astype(F32)
            total = jnp.zeros((reqs, drafts, width), F32)
            for o in range(CONV):
                tap = taps[o : o + 1]
                total = total + ext[c, :, pl.ds(EXT0 + o, drafts), at] * tap
            acts.append(total * jax.nn.sigmoid(total))
        for g in range(group):
            h = i * group + g
            mine = slice(g * DK, (g + 1) * DK)
            q = unit(acts[0][:, :, mine]) * DK ** (-0.5)
            k = unit(acts[1][:, :, mine])
            v = acts[2][:, :, mine]
            rate = jnp.sum(jnp.where(head_of == h, beta[...], 0.0), axis=-1, keepdims=True)
            rate = rate.reshape(reqs, drafts, 1)
            kh, kl = split(k)
            qh = q.astype(BF16)
            stacked = jnp.concatenate([kh, kl, qh], axis=1)
            recalled = []
            seen = []
            for r in range(reqs):
                got = jnp.dot(stacked[r], st[r, h], preferred_element_type=F32)
                recalled.append(got[:drafts] + got[drafts : 2 * drafts])
                seen.append(got[2 * drafts :])
            u = rate * (v - jnp.stack(recalled))
            k0, k1 = k[:, :half], k[:, half:]
            rate0, rate1 = rate[:, :half], rate[:, half:]
            u0, u1 = u[:, :half], u[:, half:]
            for s in range(drafts - 1):
                if s < half:
                    key_s, u_s = k0[:, s : s + 1], u0[:, s : s + 1]
                else:
                    key_s, u_s = k1[:, s - half : s - half + 1], u1[:, s - half : s - half + 1]
                if s < half - 1:
                    near = jnp.sum(k0 * key_s, axis=-1, keepdims=True) * rate0
                    u0 = u0 - jnp.where(t_half > s, near, 0.0) * u_s
                near = jnp.sum(k1 * key_s, axis=-1, keepdims=True) * rate1
                if s >= half:
                    near = jnp.where(t_half + half > s, near, 0.0)
                u1 = u1 - near * u_s
            u = jnp.concatenate([u0, u1], axis=1)
            uh = u.astype(BF16)
            near = lax.dot_general(
                qh.reshape(rows, DK),
                kh.reshape(rows, DK),
                (((1,), (1,)), ((), ())),
                preferred_element_type=F32,
            )
            near = jnp.where(causal, near, 0.0).astype(BF16)
            o = jnp.stack(seen).reshape(rows, DK) + jnp.dot(
                near, uh.reshape(rows, DK), preferred_element_type=F32
            )
            scale = lax.rsqrt(jnp.mean(o * o, axis=-1, keepdims=True) + 1e-06)
            on[:, pl.ds(pl.multiple_of(h * DK, DK), DK)] = (o * scale * out_gain).astype(BF16)
            mh, ml = split(u * kept)
            kc[h] = jnp.concatenate([kh, kl, kh], axis=1)
            uc[h] = jnp.concatenate([mh, mh, ml], axis=1)
        return 0

    lax.fori_loop(0, tiles, tile, 0)

    wo_copy.wait()
    sums = []
    for j in list(range(1, n_tp)) + [0]:
        to = lax.rem(mt + j, n_tp)
        at = pl.ds(pl.multiple_of(to * cols, cols), cols)
        part[j] = jnp.dot(on[...], wo[:, at], preferred_element_type=F32).astype(BF16)
        if j:
            copy = pltpu.make_async_remote_copy(
                src_ref=part.at[j],
                dst_ref=part_in.at[j],
                send_sem=rs_send.at[j],
                recv_sem=rs_recv.at[j],
                device_id={"tp": to},
                device_id_type=MESH,
            )
            copy.start()
            sums.append(copy)
    mine = pl.ds(pl.multiple_of(mt * cols, cols), cols)
    total = part[0].astype(F32)
    for copy in sums:
        copy.wait()
    for j in range(1, n_tp):
        total = total + part_in[j].astype(F32)
    total = xs[:, :, mine].astype(F32) + total.reshape(reqs, drafts, cols)
    done[...] = jnp.where(live > 0, total, 0.0).astype(BF16)
    for k in range(MOVE):
        back_l[k] = done[back_to_l[k]]
        back_r[k] = done[back_to_r[k]]
    returns = exchange(back_l, back_r, back, ret_send, ret_recv)

    back[pl.ds(0, reqs)] = done[...]

    def page_copy(h):
        return pltpu.make_async_copy(st.at[:, h], pages_hbm.at[:, h], out_sem.at[h])

    def accept(h, _):
        for r in range(reqs):
            gained = lax.dot_general(
                kc[h, r], uc[h, r], (((0,), (0,)), ((), ())), preferred_element_type=F32
            )
            st[r, h] = (st[r, h].astype(F32) + gained).astype(BF16)
        page_copy(h).start()
        return 0

    lax.fori_loop(0, heads, accept, 0)
    line_of = lax.broadcasted_iota(jnp.int32, (reqs, 8 + drafts, 1), 1)
    req_line = lax.broadcasted_iota(jnp.int32, (reqs, 8 + drafts, 1), 0)
    first = jnp.zeros((reqs, 8 + drafts, 1), jnp.int32)
    for j in range(reqs):
        first = jnp.where(req_line == j, EXT0 + keeps[j], first)

    def edges(c, _):
        for e in range(HIST):
            chosen = jnp.where(line_of == first + e, ext[c], 0.0)
            fconv_ref[e, c] = jnp.sum(chosen, axis=1).astype(BF16)
        return 0

    lax.fori_loop(0, 3, edges, 0)

    for copy in returns:
        copy.wait()
    for i in range(reqs):
        mixed_ref[i] = back[homes[i]]

    def drain(h, _):
        page_copy(h).wait()
        return 0

    lax.fori_loop(0, heads, drain, 0)


def on_device(
    n_seq,
    n_tp,
    tokens,
    gain_in,
    w_qkv,
    w_beta,
    conv_weight,
    out_gain,
    w_out,
    state_pages,
    conv_pages,
    page_order,
    draft_lengths,
    accepted,
):
    reqs, drafts, cols = tokens.shape
    rows = reqs * drafts
    depth = w_qkv.shape[1]
    heads = state_pages.shape[1]
    hidden = heads * DK
    smem = pl.BlockSpec(memory_space=pltpu.SMEM)
    vmem = pl.BlockSpec(memory_space=pltpu.VMEM)
    hbm = pl.BlockSpec(memory_space=pl.ANY)
    dma = pltpu.SemaphoreType.DMA
    mixed, final_conv, pages = pl.pallas_call(
        functools.partial(kernel, n_seq, n_tp),
        out_shape=(
            jax.ShapeDtypeStruct(tokens.shape, BF16),
            jax.ShapeDtypeStruct((HIST, 3, reqs, hidden), BF16),
            jax.ShapeDtypeStruct(state_pages.shape, BF16),
        ),
        in_specs=[smem] * 3 + [vmem] * 6 + [hbm] * 3,
        out_specs=(vmem, vmem, hbm),
        scratch_shapes=[
            pltpu.VMEM(w_qkv.shape, BF16),
            pltpu.VMEM(w_out.shape, BF16),
            pltpu.VMEM(state_pages.shape, BF16),
            pltpu.VMEM((n_tp, reqs + 2 * MOVE, drafts, cols), BF16),
            pltpu.VMEM((MOVE, drafts, cols), BF16),
            pltpu.VMEM((MOVE, drafts, cols), BF16),
            pltpu.VMEM((reqs, drafts, depth), BF16),
            pltpu.VMEM((rows, depth), BF16),
            pltpu.VMEM((3, reqs, 8 + drafts, hidden), F32),
            pltpu.VMEM((rows, heads), F32),
            pltpu.VMEM((rows, hidden), BF16),
            pltpu.VMEM((heads, reqs, 3 * drafts, DK), BF16),
            pltpu.VMEM((heads, reqs, 3 * drafts, DK), BF16),
            pltpu.VMEM((n_tp, rows, cols), BF16),
            pltpu.VMEM((n_tp, rows, cols), BF16),
            pltpu.VMEM(tokens.shape, BF16),
            pltpu.VMEM((reqs + 2 * MOVE, drafts, cols), BF16),
            pltpu.VMEM((MOVE, drafts, cols), BF16),
            pltpu.VMEM((MOVE, drafts, cols), BF16),
            dma((heads,)),
            dma,
            dma,
            dma((heads,)),
            dma((2,)),
            dma((2,)),
            dma((2, n_tp)),
            dma((2, n_tp)),
            dma((n_tp,)),
            dma((n_tp,)),
            dma((2,)),
            dma((2,)),
        ],
        compiler_params=pltpu.CompilerParams(
            collective_id=0, has_side_effects=True, vmem_limit_bytes=52 * 1024 * 1024
        ),
    )(
        page_order,
        draft_lengths,
        accepted,
        tokens,
        gain_in.reshape(1, -1),
        w_beta.T,
        jnp.transpose(conv_weight, (1, 0, 2)),
        out_gain.reshape(1, -1),
        jnp.transpose(conv_pages, (1, 2, 0, 3)),
        w_qkv,
        w_out,
        state_pages,
    )
    return mixed, pages, jnp.transpose(final_conv, (2, 0, 1, 3))


def solution(mesh):
    return jax.shard_map(
        functools.partial(on_device, mesh.shape["seq"], mesh.shape["tp"]),
        mesh=mesh,
        in_specs=(
            P("seq", None, "tp"),
            P(),
            P(None, None, "tp"),
            P(None, "tp"),
            P(None, None, "tp"),
            P(),
            P("tp", None),
            P("seq", "tp", None, None),
            P("seq", None, None, "tp"),
            P(),
            P(),
            P(),
        ),
        out_specs=(P("seq", None, "tp"), P("seq", "tp", None, None), P("seq", None, None, "tp")),
        check_vma=False,
    )
```

```python
import functools

import jax
import jax.numpy as jnp
from jax import lax
from jax.experimental import pallas as pl
from jax.experimental.pallas import tpu as pltpu
from jax.sharding import PartitionSpec as P

DK = 128
CONV = 4
MOVE = 4
HIST = CONV - 1
EXT0 = 8 - HIST
F32 = jnp.float32
BF16 = jnp.bfloat16
MESH = pl.DeviceIdType.MESH


def split(wide):
    high = wide.astype(BF16)
    return high, (wide - high.astype(F32)).astype(BF16)


def unit(values):
    return values * lax.rsqrt(jnp.sum(values * values, axis=-1, keepdims=True) + 1e-06)


def matches(po_ref, device, home, reqs):
    found = []
    count = jnp.int32(0)
    for j in range(reqs):
        request = po_ref[device * reqs + j]
        hit = (request >= home * reqs) & (request < home * reqs + reqs)
        found.append((request, hit, count))
        count = count + hit.astype(jnp.int32)
    return found


def pick_rank(found, rank, values):
    total = jnp.int32(0)
    for (_, hit, place), value in zip(found, values):
        total = total + jnp.where(hit & (place == rank), value, 0)
    return jnp.clip(total, 0, len(values) - 1)


def kernel(
    n_seq,
    n_tp,
    po_hbm,
    len_hbm,
    acc_hbm,
    tok_hbm,
    gain_hbm,
    wb_hbm,
    cw_hbm,
    og_hbm,
    conv_hbm,
    wqkv_hbm,
    wout_hbm,
    state_hbm,
    mixed_ref,
    fconv_ref,
    pages_hbm,
    po_ref,
    len_ref,
    acc_ref,
    tok_ref,
    gain_ref,
    wb_ref,
    cw_ref,
    og_ref,
    conv_ref,
    wq,
    wo,
    st,
    pool,
    send_l,
    send_r,
    xs,
    normed,
    ext,
    queries,
    keys,
    values,
    beta,
    on,
    kc,
    uc,
    part,
    part_in,
    done,
    back,
    pages_ref,
    in_sem,
    out_sem,
    w_sem,
    wo_sem,
    st_sem,
    mig_send,
    mig_recv,
    tp_send,
    tp_recv,
    rs_send,
    rs_recv,
    ret_send,
    ret_recv,
):
    reqs, drafts, cols = tok_ref.shape
    rows = reqs * drafts
    heads = state_hbm.shape[1]
    hidden = heads * DK
    group = 2 if heads % 2 == 0 else 1
    width = group * DK
    tiles = heads // group
    me = lax.axis_index("seq")
    mt = lax.axis_index("tp")
    left = lax.rem(me + n_seq - 1, n_seq)
    right = lax.rem(me + 1, n_seq)

    def w_copy(i):
        at = pl.ds(pl.multiple_of(i * width, width), width)
        return pltpu.make_async_copy(wqkv_hbm.at[:, :, at], wq.at[:, :, at], w_sem.at[i])

    st_copy = pltpu.make_async_copy(state_hbm, st, st_sem)
    wo_copy = pltpu.make_async_copy(wout_hbm, wo, wo_sem)
    small = []
    pairs = (
        (po_hbm, po_ref),
        (len_hbm, len_ref),
        (acc_hbm, acc_ref),
        (tok_hbm, tok_ref),
        (conv_hbm, conv_ref),
        (gain_hbm, gain_ref),
        (wb_hbm, wb_ref),
        (cw_hbm, cw_ref),
        (og_hbm, og_ref),
    )
    for i, (src, dst) in enumerate(pairs):
        small.append(pltpu.make_async_copy(src, dst, in_sem.at[i]))
        small[i].start()
    w_copy(0).start()
    st_copy.start()
    for i in range(1, tiles):
        w_copy(i).start()
    wo_copy.start()

    barrier = pltpu.get_barrier_semaphore()
    for other in (left, right):
        pl.semaphore_signal(barrier, inc=1, device_id={"seq": other}, device_id_type=MESH)
    for j in range(1, n_tp):
        pl.semaphore_signal(
            barrier, inc=1, device_id={"tp": lax.rem(mt + j, n_tp)}, device_id_type=MESH
        )

    for copy in small[:4]:
        copy.wait()
    own = matches(po_ref, me, me, reqs)
    from_l = matches(po_ref, me, left, reqs)
    from_r = matches(po_ref, me, right, reqs)
    at_l = matches(po_ref, left, me, reqs)
    at_r = matches(po_ref, right, me, reqs)
    base = me * reqs
    for k in range(MOVE):
        send_l[k] = tok_ref[pick_rank(at_l, k, [f[0] - base for f in at_l])]
        send_r[k] = tok_ref[pick_rank(at_r, k, [f[0] - base for f in at_r])]
    pl.semaphore_wait(barrier, 2 + n_tp - 1)

    def to_right(src, dst, send_sem, recv_sem):
        copy = pltpu.make_async_remote_copy(
            src_ref=src,
            dst_ref=dst.at[pl.ds(reqs, MOVE)],
            send_sem=send_sem.at[0],
            recv_sem=recv_sem.at[0],
            device_id={"seq": right},
            device_id_type=MESH,
        )
        copy.start()
        return copy

    def to_left(src, dst, send_sem, recv_sem):
        copy = pltpu.make_async_remote_copy(
            src_ref=src,
            dst_ref=dst.at[pl.ds(reqs + MOVE, MOVE)],
            send_sem=send_sem.at[1],
            recv_sem=recv_sem.at[1],
            device_id={"seq": left},
            device_id_type=MESH,
        )
        copy.start()
        return copy

    moves = [
        to_right(send_r, pool.at[mt], mig_send, mig_recv),
        to_left(send_l, pool.at[mt], mig_send, mig_recv),
    ]

    def to_peers(src, dst, stage):
        copies = []
        for j in range(1, n_tp):
            copy = pltpu.make_async_remote_copy(
                src_ref=src,
                dst_ref=dst,
                send_sem=tp_send.at[stage, j],
                recv_sem=tp_recv.at[stage, j],
                device_id={"tp": lax.rem(mt + j, n_tp)},
                device_id_type=MESH,
            )
            copy.start()
            copies.append(copy)
        return copies

    gathers = to_peers(tok_ref, pool.at[mt, pl.ds(0, reqs)], 0)
    pool[mt, pl.ds(0, reqs)] = tok_ref[...]

    count_l = jnp.int32(0)
    count_r = jnp.int32(0)
    for j in range(reqs):
        count_l = count_l + from_l[j][1].astype(jnp.int32)
        count_r = count_r + from_r[j][1].astype(jnp.int32)
    spot = []
    places = []
    for j in range(reqs):
        rank = own[j][2]
        room = MOVE - count_l
        here = jnp.where(rank < room, count_l + rank, MOVE + count_r + rank - room)
        other = jnp.where(from_l[j][1], from_l[j][2], MOVE + from_r[j][2])
        spot.append(jnp.clip(jnp.where(own[j][1], here, other), 0, reqs - 1))
        place = jnp.where(from_l[j][1], reqs + from_l[j][2], reqs + MOVE + from_r[j][2])
        place = jnp.where(own[j][1], own[j][0] - base, place)
        places.append(jnp.clip(place, 0, reqs + 2 * MOVE - 1))
    slot_at = []
    place_at = []
    lengths = []
    keeps = []
    for p in range(reqs):
        slot = jnp.int32(0)
        place = jnp.int32(0)
        request = jnp.int32(0)
        for j in range(reqs):
            hit = spot[j] == p
            slot = jnp.where(hit, j, slot)
            place = jnp.where(hit, places[j], place)
            request = jnp.where(hit, own[j][0], request)
        slot_at.append(slot)
        place_at.append(place)
        lengths.append(len_ref[request])
        keeps.append(jnp.minimum(acc_ref[request], lengths[p]))
    homes = []
    for i in range(reqs):
        place = jnp.int32(0)
        for j in range(reqs):
            place = jnp.where(own[j][0] == base + i, spot[j], place)
            place = jnp.where(at_l[j][0] == base + i, reqs + at_l[j][2], place)
            place = jnp.where(at_r[j][0] == base + i, reqs + MOVE + at_r[j][2], place)
        homes.append(jnp.clip(place, 0, reqs + 2 * MOVE - 1))

    def spread(numbers, shape):
        index = lax.broadcasted_iota(jnp.int32, shape, 0)
        out = jnp.zeros(shape, jnp.int32)
        for p in range(reqs):
            out = jnp.where(index == p, numbers[p], out)
        return out

    step_of = lax.broadcasted_iota(jnp.int32, (reqs, drafts, 1), 1)
    live = (step_of < spread(lengths, (reqs, drafts, 1))).astype(F32)
    kept = (step_of < spread(keeps, (reqs, drafts, 1))).astype(F32)
    lane_of = lax.broadcasted_iota(jnp.int32, (reqs, reqs), 1)
    to_spot = (lane_of == spread(slot_at, (reqs, reqs))).astype(F32).astype(BF16)
    to_slot = (lane_of == spread(spot, (reqs, reqs))).astype(F32).astype(BF16)
    for copy in small[4:]:
        copy.wait()
    for e in range(HIST):
        for c in range(3):
            ext[c, :, EXT0 + e, :] = jnp.dot(
                to_spot, conv_ref[e, c], preferred_element_type=F32
            )

    for copy in moves:
        copy.wait()
    gathers += to_peers(
        pool.at[mt, pl.ds(reqs, 2 * MOVE)], pool.at[mt, pl.ds(reqs, 2 * MOVE)], 1
    )
    for copy in gathers:
        copy.wait()

    gain = gain_ref[...].astype(F32).reshape(1, -1)
    for j in range(reqs):
        for c in range(n_tp):
            xs[j, :, pl.ds(c * cols, cols)] = pool[c, place_at[j]]
        wide = xs[j].astype(F32)
        scale = lax.rsqrt(jnp.mean(wide * wide, axis=-1, keepdims=True) + 1e-06)
        normed[pl.ds(j * drafts, drafts), :] = (wide * scale * gain).astype(BF16)
    rates = jax.nn.sigmoid(
        lax.dot_general(
            normed[...], wb_ref[...], (((1,), (1,)), ((), ())), preferred_element_type=F32
        )
    )
    beta[...] = rates * live.reshape(rows, 1)

    many = group * MOVE
    block = many * drafts
    row_of = lax.broadcasted_iota(jnp.int32, (block, block), 0)
    col_of = lax.broadcasted_iota(jnp.int32, (block, block), 1)
    causal = (row_of // drafts == col_of // drafts) & (col_of <= row_of)
    half = drafts // 2
    t_half = lax.broadcasted_iota(jnp.int32, (1, half, 1), 1)
    head_of = lax.broadcasted_iota(jnp.int32, (MOVE * drafts, heads), 1)
    out_gain = og_ref[...].astype(F32)

    def tile(i, _):
        at = pl.ds(pl.multiple_of(i * width, width), width)
        w_copy(i).wait()
        acts = []
        for c in range(3):
            proj = jnp.dot(normed[...], wq[c, :, at], preferred_element_type=F32)
            ext[c, :, pl.ds(8, drafts), at] = (
                proj.astype(BF16).astype(F32).reshape(reqs, drafts, width)
            )
            taps = cw_ref[c, :, at].astype(F32)
            total = jnp.zeros((reqs, drafts, width), F32)
            for o in range(CONV):
                tap = taps[o : o + 1]
                total = total + ext[c, :, pl.ds(EXT0 + o, drafts), at] * tap
            acts.append(total * jax.nn.sigmoid(total))
        for g in range(group):
            h = i * group + g
            mine = slice(g * DK, (g + 1) * DK)
            queries[h] = (unit(acts[0][:, :, mine]) * DK ** (-0.5)).astype(BF16)
            keys[h] = unit(acts[1][:, :, mine])
            values[h] = acts[2][:, :, mine]
        return 0

    lax.fori_loop(0, tiles, tile, 0)
    st_copy.wait()

    def delta(side):
        mine = pl.ds(side * MOVE, MOVE)
        kept_here = kept[side * MOVE : (side + 1) * MOVE]

        def heads_of(i, _):
            at = pl.ds(i * group, group)
            q = queries[at, mine].reshape(many, drafts, DK)
            k = keys[at, mine].reshape(many, drafts, DK)
            v = values[at, mine].reshape(many, drafts, DK)
            rate = []
            for g in range(group):
                rates = beta[pl.ds(side * MOVE * drafts, MOVE * drafts), :]
                rate.append(
                    jnp.sum(
                        jnp.where(head_of == i * group + g, rates, 0.0), axis=-1, keepdims=True
                    ).reshape(MOVE, drafts, 1)
                )
            rate = jnp.concatenate(rate, axis=0)
            kh, kl = split(k)
            stacked = jnp.concatenate([kh, kl, q], axis=1)
            recalled = []
            seen = []
            for g in range(group):
                for r in range(MOVE):
                    state = st[slot_at[side * MOVE + r], i * group + g]
                    got = jnp.dot(stacked[g * MOVE + r], state, preferred_element_type=F32)
                    recalled.append(got[:drafts] + got[drafts : 2 * drafts])
                    seen.append(got[2 * drafts :])
            u = rate * (v - jnp.stack(recalled))
            k0, k1 = k[:, :half], k[:, half:]
            rate0, rate1 = rate[:, :half], rate[:, half:]
            u0, u1 = u[:, :half], u[:, half:]
            for s in range(drafts - 1):
                if s < half:
                    key_s, u_s = k0[:, s : s + 1], u0[:, s : s + 1]
                else:
                    key_s, u_s = k1[:, s - half : s - half + 1], u1[:, s - half : s - half + 1]
                if s < half - 1:
                    near = jnp.sum(k0 * key_s, axis=-1, keepdims=True) * rate0
                    u0 = u0 - jnp.where(t_half > s, near, 0.0) * u_s
                near = jnp.sum(k1 * key_s, axis=-1, keepdims=True) * rate1
                if s >= half:
                    near = jnp.where(t_half + half > s, near, 0.0)
                u1 = u1 - near * u_s
            u = jnp.concatenate([u0, u1], axis=1)
            near = lax.dot_general(
                q.reshape(block, DK),
                kh.reshape(block, DK),
                (((1,), (1,)), ((), ())),
                preferred_element_type=F32,
            )
            near = jnp.where(causal, near, 0.0).astype(BF16)
            o = jnp.stack(seen).reshape(block, DK) + jnp.dot(
                near, u.astype(BF16).reshape(block, DK), preferred_element_type=F32
            )
            scale = lax.rsqrt(jnp.mean(o * o, axis=-1, keepdims=True) + 1e-06)
            o = (o * scale * out_gain).astype(BF16)
            rows_here = MOVE * drafts
            for g in range(group):
                columns = pl.ds(pl.multiple_of((i * group + g) * DK, DK), DK)
                on[pl.ds(side * rows_here, rows_here), columns] = o[
                    g * rows_here : (g + 1) * rows_here
                ]
            u = u.reshape(group, MOVE, drafts, DK) * kept_here[None]
            mh, ml = split(u.reshape(many, drafts, DK))
            shape = (group, MOVE, 3 * drafts, DK)
            kc[at, mine] = jnp.concatenate([kh, kl, kh], axis=1).reshape(shape)
            uc[at, mine] = jnp.concatenate([mh, mh, ml], axis=1).reshape(shape)
            return 0

        return heads_of

    def project(side):
        sums = []
        lines = pl.ds(side * MOVE * drafts, MOVE * drafts)
        for j in list(range(1, n_tp)) + [0]:
            to = lax.rem(mt + j, n_tp)
            at = pl.ds(pl.multiple_of(to * cols, cols), cols)
            part[side, j] = jnp.dot(
                on[lines, :], wo[:, at], preferred_element_type=F32
            ).astype(BF16)
            if j:
                copy = pltpu.make_async_remote_copy(
                    src_ref=part.at[side, j],
                    dst_ref=part_in.at[side, j],
                    send_sem=rs_send.at[side, j],
                    recv_sem=rs_recv.at[side, j],
                    device_id={"tp": to},
                    device_id_type=MESH,
                )
                copy.start()
                sums.append(copy)
        return sums

    def finish(side, sums):
        for copy in sums:
            copy.wait()
        total = part[side, 0].astype(F32)
        for j in range(1, n_tp):
            total = total + part_in[side, j].astype(F32)
        mine = pl.ds(side * MOVE, MOVE)
        columns = pl.ds(pl.multiple_of(mt * cols, cols), cols)
        total = xs[mine, :, columns].astype(F32) + total.reshape(MOVE, drafts, cols)
        live_here = live[side * MOVE : (side + 1) * MOVE]
        rows_done = jnp.where(live_here > 0, total, 0.0).astype(BF16)
        done[mine] = rows_done
        back[mine] = rows_done

    lax.fori_loop(0, tiles, delta(0), 0)
    wo_copy.wait()
    sums = project(0)
    second = delta(1)
    lax.fori_loop(0, 1, second, 0)
    finish(0, sums)
    returns = [to_left(done.at[pl.ds(0, MOVE)], back, ret_send, ret_recv)]
    lax.fori_loop(1, tiles, second, 0)
    sums = project(1)

    line_of = lax.broadcasted_iota(jnp.int32, (reqs, 8 + drafts, 1), 1)
    first = EXT0 + spread(keeps, (reqs, 8 + drafts, 1))

    def edges(c, _):
        for e in range(HIST):
            chosen = jnp.sum(jnp.where(line_of == first + e, ext[c], 0.0), axis=1)
            fconv_ref[e, c] = jnp.dot(
                to_slot, chosen.astype(BF16), preferred_element_type=F32
            ).astype(BF16)
        return 0

    lax.fori_loop(0, 3, edges, 0)
    finish(1, sums)
    returns.append(to_right(done.at[pl.ds(MOVE, MOVE)], back, ret_send, ret_recv))

    def page_copy(h):
        return pltpu.make_async_copy(pages_ref.at[:, h], pages_hbm.at[:, h], out_sem.at[h])

    def accept(h, _):
        for j in range(reqs):
            gained = lax.dot_general(
                kc[h, spot[j]], uc[h, spot[j]], (((0,), (0,)), ((), ())), preferred_element_type=F32
            )
            pages_ref[j, h] = (st[j, h].astype(F32) + gained).astype(BF16)
        page_copy(h).start()
        return 0

    def drain(h, _):
        page_copy(h).wait()
        return 0

    lax.fori_loop(0, heads, accept, 0)
    for copy in returns:
        copy.wait()
    for i in range(reqs):
        mixed_ref[i] = back[homes[i]]
    lax.fori_loop(0, heads, drain, 0)


def hand_out(mixed_in, fconv_in, pages_in, mixed_out, fconv_out, pages_out, sem):
    reqs = pages_in.shape[0]
    copies = [
        pltpu.make_async_copy(mixed_in, mixed_out, sem.at[reqs]),
        pltpu.make_async_copy(fconv_in, fconv_out, sem.at[reqs + 1]),
    ]
    for j in range(reqs):
        copies.append(pltpu.make_async_copy(pages_in.at[j], pages_out.at[j], sem.at[j]))
    for copy in copies:
        copy.start()
    for copy in copies:
        copy.wait()


def on_device(
    n_seq,
    n_tp,
    tokens,
    gain_in,
    w_qkv,
    w_beta,
    conv_weight,
    out_gain,
    w_out,
    state_pages,
    conv_pages,
    page_order,
    draft_lengths,
    accepted,
):
    reqs, drafts, cols = tokens.shape
    rows = reqs * drafts
    depth = w_qkv.shape[1]
    heads = state_pages.shape[1]
    hidden = heads * DK
    vmem = pl.BlockSpec(memory_space=pltpu.VMEM)
    hbm = pl.BlockSpec(memory_space=pltpu.HBM)
    dma = pltpu.SemaphoreType.DMA
    results = pl.pallas_call(
        functools.partial(kernel, n_seq, n_tp),
        out_shape=(
            jax.ShapeDtypeStruct(tokens.shape, BF16),
            jax.ShapeDtypeStruct((HIST, 3, reqs, hidden), BF16),
            jax.ShapeDtypeStruct(state_pages.shape, BF16),
        ),
        in_specs=[hbm] * 12,
        out_specs=(vmem, vmem, hbm),
        scratch_shapes=[
            pltpu.SMEM(page_order.shape, jnp.int32),
            pltpu.SMEM(draft_lengths.shape, jnp.int32),
            pltpu.SMEM(accepted.shape, jnp.int32),
            pltpu.VMEM(tokens.shape, BF16),
            pltpu.VMEM(gain_in.shape, BF16),
            pltpu.VMEM((heads, depth), BF16),
            pltpu.VMEM((3, CONV, hidden), BF16),
            pltpu.VMEM((1, DK), BF16),
            pltpu.VMEM((HIST, 3, reqs, hidden), BF16),
            pltpu.VMEM(w_qkv.shape, BF16),
            pltpu.VMEM(w_out.shape, BF16),
            pltpu.VMEM(state_pages.shape, BF16),
            pltpu.VMEM((n_tp, reqs + 2 * MOVE, drafts, cols), BF16),
            pltpu.VMEM((MOVE, drafts, cols), BF16),
            pltpu.VMEM((MOVE, drafts, cols), BF16),
            pltpu.VMEM((reqs, drafts, depth), BF16),
            pltpu.VMEM((rows, depth), BF16),
            pltpu.VMEM((3, reqs, 8 + drafts, hidden), F32),
            pltpu.VMEM((heads, reqs, drafts, DK), BF16),
            pltpu.VMEM((heads, reqs, drafts, DK), F32),
            pltpu.VMEM((heads, reqs, drafts, DK), F32),
            pltpu.VMEM((rows, heads), F32),
            pltpu.VMEM((rows, hidden), BF16),
            pltpu.VMEM((heads, reqs, 3 * drafts, DK), BF16),
            pltpu.VMEM((heads, reqs, 3 * drafts, DK), BF16),
            pltpu.VMEM((2, n_tp, MOVE * drafts, cols), BF16),
            pltpu.VMEM((2, n_tp, MOVE * drafts, cols), BF16),
            pltpu.VMEM(tokens.shape, BF16),
            pltpu.VMEM((reqs + 2 * MOVE, drafts, cols), BF16),
            pltpu.VMEM(state_pages.shape, BF16),
            dma((9,)),
            dma((heads,)),
            dma((heads,)),
            dma,
            dma,
            dma((2,)),
            dma((2,)),
            dma((2, n_tp)),
            dma((2, n_tp)),
            dma((2, n_tp)),
            dma((2, n_tp)),
            dma((2,)),
            dma((2,)),
        ],
        compiler_params=pltpu.CompilerParams(
            collective_id=0, has_side_effects=True, vmem_limit_bytes=60 * 1024 * 1024
        ),
    )(
        page_order,
        draft_lengths,
        accepted,
        tokens,
        gain_in,
        w_beta.T,
        jnp.transpose(conv_weight, (1, 0, 2)),
        out_gain.reshape(1, -1),
        jnp.transpose(conv_pages, (1, 2, 0, 3)),
        w_qkv,
        w_out,
        state_pages,
    )
    mixed, final_conv, pages = pl.pallas_call(
        hand_out,
        out_shape=tuple(jax.ShapeDtypeStruct(a.shape, a.dtype) for a in results),
        in_specs=[hbm] * 3,
        out_specs=(hbm,) * 3,
        scratch_shapes=[dma((reqs + 2,))],
        compiler_params=pltpu.CompilerParams(vmem_limit_bytes=60 * 1024 * 1024),
    )(*results)
    return mixed, pages, jnp.transpose(final_conv, (2, 0, 1, 3))


def solution(mesh):
    return jax.shard_map(
        functools.partial(on_device, mesh.shape["seq"], mesh.shape["tp"]),
        mesh=mesh,
        in_specs=(
            P("seq", None, "tp"),
            P(),
            P(None, None, "tp"),
            P(None, "tp"),
            P(None, None, "tp"),
            P(),
            P("tp", None),
            P("seq", "tp", None, None),
            P("seq", None, None, "tp"),
            P(),
            P(),
            P(),
        ),
        out_specs=(P("seq", None, "tp"), P("seq", "tp", None, None), P("seq", None, None, "tp")),
        check_vma=False,
    )
```

```python
import functools

import jax
import jax.numpy as jnp
from jax import lax
from jax.experimental import pallas as pl
from jax.experimental.pallas import tpu as pltpu
from jax.sharding import PartitionSpec as P

DK = 128
CONV = 4
MOVE = 4
HIST = CONV - 1
EXT0 = 8 - HIST
F32 = jnp.float32
BF16 = jnp.bfloat16
MESH = pl.DeviceIdType.MESH


def split(wide):
    high = wide.astype(BF16)
    return high, (wide - high.astype(F32)).astype(BF16)


def unit(values):
    return values * lax.rsqrt(jnp.sum(values * values, axis=-1, keepdims=True) + 1e-06)


def matches(po_ref, device, home, reqs):
    found = []
    count = jnp.int32(0)
    for j in range(reqs):
        request = po_ref[device * reqs + j]
        hit = (request >= home * reqs) & (request < home * reqs + reqs)
        found.append((request, hit, count))
        count = count + hit.astype(jnp.int32)
    return found


def pick_rank(found, rank, values):
    total = jnp.int32(0)
    for (_, hit, place), value in zip(found, values):
        total = total + jnp.where(hit & (place == rank), value, 0)
    return jnp.clip(total, 0, len(values) - 1)


def kernel(
    n_seq,
    n_tp,
    po_hbm,
    len_hbm,
    acc_hbm,
    tok_hbm,
    gain_hbm,
    wb_hbm,
    cw_hbm,
    og_hbm,
    conv_hbm,
    wqkv_hbm,
    wout_hbm,
    state_hbm,
    mixed_ref,
    fconv_ref,
    pages_hbm,
    po_ref,
    len_ref,
    acc_ref,
    tok_ref,
    gain_ref,
    wb_ref,
    cw_ref,
    og_ref,
    conv_ref,
    wq,
    wo,
    st,
    pool,
    send_l,
    send_r,
    xs,
    normed,
    ext,
    queries,
    keys,
    values,
    beta,
    on,
    kc,
    uc,
    part,
    part_in,
    done,
    back,
    pages_ref,
    in_sem,
    out_sem,
    w_sem,
    wo_sem,
    st_sem,
    mig_send,
    mig_recv,
    tp_send,
    tp_recv,
    rs_send,
    rs_recv,
    ret_send,
    ret_recv,
):
    reqs, drafts, cols = tok_ref.shape
    rows = reqs * drafts
    heads = state_hbm.shape[1]
    hidden = heads * DK
    group = 2 if heads % 2 == 0 else 1
    width = group * DK
    tiles = heads // group
    me = lax.axis_index("seq")
    mt = lax.axis_index("tp")
    left = lax.rem(me + n_seq - 1, n_seq)
    right = lax.rem(me + 1, n_seq)

    def w_copy(i):
        at = pl.ds(pl.multiple_of(i * width, width), width)
        return pltpu.make_async_copy(wqkv_hbm.at[:, :, at], wq.at[:, :, at], w_sem.at[i])

    st_copy = pltpu.make_async_copy(state_hbm, st, st_sem)
    wo_copy = pltpu.make_async_copy(wout_hbm, wo, wo_sem)
    small = []
    pairs = (
        (po_hbm, po_ref),
        (len_hbm, len_ref),
        (acc_hbm, acc_ref),
        (tok_hbm, tok_ref),
        (conv_hbm, conv_ref),
        (gain_hbm, gain_ref),
        (wb_hbm, wb_ref),
        (cw_hbm, cw_ref),
        (og_hbm, og_ref),
    )
    for i, (src, dst) in enumerate(pairs):
        small.append(pltpu.make_async_copy(src, dst, in_sem.at[i]))
        small[i].start()
    w_copy(0).start()
    st_copy.start()
    for i in range(1, tiles):
        w_copy(i).start()
    wo_copy.start()

    barrier = pltpu.get_barrier_semaphore()
    for other in (left, right):
        pl.semaphore_signal(barrier, inc=1, device_id={"seq": other}, device_id_type=MESH)
    for j in range(1, n_tp):
        pl.semaphore_signal(
            barrier, inc=1, device_id={"tp": lax.rem(mt + j, n_tp)}, device_id_type=MESH
        )

    for copy in small[:4]:
        copy.wait()
    own = matches(po_ref, me, me, reqs)
    from_l = matches(po_ref, me, left, reqs)
    from_r = matches(po_ref, me, right, reqs)
    at_l = matches(po_ref, left, me, reqs)
    at_r = matches(po_ref, right, me, reqs)
    base = me * reqs
    for k in range(MOVE):
        send_l[k] = tok_ref[pick_rank(at_l, k, [f[0] - base for f in at_l])]
        send_r[k] = tok_ref[pick_rank(at_r, k, [f[0] - base for f in at_r])]
    pl.semaphore_wait(barrier, 2 + n_tp - 1)

    def to_right(src, dst, send_sem, recv_sem):
        copy = pltpu.make_async_remote_copy(
            src_ref=src,
            dst_ref=dst.at[pl.ds(reqs, MOVE)],
            send_sem=send_sem.at[0],
            recv_sem=recv_sem.at[0],
            device_id={"seq": right},
            device_id_type=MESH,
        )
        copy.start()
        return copy

    def to_left(src, dst, send_sem, recv_sem):
        copy = pltpu.make_async_remote_copy(
            src_ref=src,
            dst_ref=dst.at[pl.ds(reqs + MOVE, MOVE)],
            send_sem=send_sem.at[1],
            recv_sem=recv_sem.at[1],
            device_id={"seq": left},
            device_id_type=MESH,
        )
        copy.start()
        return copy

    moves = [
        to_right(send_r, pool.at[mt], mig_send, mig_recv),
        to_left(send_l, pool.at[mt], mig_send, mig_recv),
    ]

    def to_peers(src, dst, stage):
        copies = []
        for j in range(1, n_tp):
            copy = pltpu.make_async_remote_copy(
                src_ref=src,
                dst_ref=dst,
                send_sem=tp_send.at[stage, j],
                recv_sem=tp_recv.at[stage, j],
                device_id={"tp": lax.rem(mt + j, n_tp)},
                device_id_type=MESH,
            )
            copy.start()
            copies.append(copy)
        return copies

    gathers = to_peers(tok_ref, pool.at[mt, pl.ds(0, reqs)], 0)
    pool[mt, pl.ds(0, reqs)] = tok_ref[...]

    count_l = jnp.int32(0)
    count_r = jnp.int32(0)
    for j in range(reqs):
        count_l = count_l + from_l[j][1].astype(jnp.int32)
        count_r = count_r + from_r[j][1].astype(jnp.int32)
    spot = []
    places = []
    for j in range(reqs):
        rank = own[j][2]
        room = MOVE - count_l
        here = jnp.where(rank < room, count_l + rank, MOVE + count_r + rank - room)
        other = jnp.where(from_l[j][1], from_l[j][2], MOVE + from_r[j][2])
        spot.append(jnp.clip(jnp.where(own[j][1], here, other), 0, reqs - 1))
        place = jnp.where(from_l[j][1], reqs + from_l[j][2], reqs + MOVE + from_r[j][2])
        place = jnp.where(own[j][1], own[j][0] - base, place)
        places.append(jnp.clip(place, 0, reqs + 2 * MOVE - 1))
    slot_at = []
    place_at = []
    lengths = []
    keeps = []
    for p in range(reqs):
        slot = jnp.int32(0)
        place = jnp.int32(0)
        request = jnp.int32(0)
        for j in range(reqs):
            hit = spot[j] == p
            slot = jnp.where(hit, j, slot)
            place = jnp.where(hit, places[j], place)
            request = jnp.where(hit, own[j][0], request)
        slot_at.append(slot)
        place_at.append(place)
        lengths.append(len_ref[request])
        keeps.append(jnp.minimum(acc_ref[request], lengths[p]))
    homes = []
    for i in range(reqs):
        place = jnp.int32(0)
        for j in range(reqs):
            place = jnp.where(own[j][0] == base + i, spot[j], place)
            place = jnp.where(at_l[j][0] == base + i, reqs + at_l[j][2], place)
            place = jnp.where(at_r[j][0] == base + i, reqs + MOVE + at_r[j][2], place)
        homes.append(jnp.clip(place, 0, reqs + 2 * MOVE - 1))

    def spread(numbers, shape):
        index = lax.broadcasted_iota(jnp.int32, shape, 0)
        out = jnp.zeros(shape, jnp.int32)
        for p in range(reqs):
            out = jnp.where(index == p, numbers[p], out)
        return out

    step_of = lax.broadcasted_iota(jnp.int32, (reqs, drafts, 1), 1)
    live = (step_of < spread(lengths, (reqs, drafts, 1))).astype(F32)
    kept = (step_of < spread(keeps, (reqs, drafts, 1))).astype(F32)
    lane_of = lax.broadcasted_iota(jnp.int32, (reqs, reqs), 1)
    to_spot = (lane_of == spread(slot_at, (reqs, reqs))).astype(F32).astype(BF16)
    to_slot = (lane_of == spread(spot, (reqs, reqs))).astype(F32).astype(BF16)
    for copy in small[4:]:
        copy.wait()
    for e in range(HIST):
        for c in range(3):
            ext[c, :, EXT0 + e, :] = jnp.dot(
                to_spot, conv_ref[e, c], preferred_element_type=F32
            )

    for copy in moves:
        copy.wait()
    gathers += to_peers(
        pool.at[mt, pl.ds(reqs, 2 * MOVE)], pool.at[mt, pl.ds(reqs, 2 * MOVE)], 1
    )
    for copy in gathers:
        copy.wait()

    gain = gain_ref[...].astype(F32).reshape(1, -1)
    for j in range(reqs):
        for c in range(n_tp):
            xs[j, :, pl.ds(c * cols, cols)] = pool[c, place_at[j]]
        wide = xs[j].astype(F32)
        scale = lax.rsqrt(jnp.mean(wide * wide, axis=-1, keepdims=True) + 1e-06)
        normed[pl.ds(j * drafts, drafts), :] = (wide * scale * gain).astype(BF16)
    rates = jax.nn.sigmoid(
        lax.dot_general(
            normed[...], wb_ref[...], (((1,), (1,)), ((), ())), preferred_element_type=F32
        )
    )
    beta[...] = rates * live.reshape(rows, 1)

    many = group * MOVE
    block = many * drafts
    row_of = lax.broadcasted_iota(jnp.int32, (block, block), 0)
    col_of = lax.broadcasted_iota(jnp.int32, (block, block), 1)
    causal = (row_of // drafts == col_of // drafts) & (col_of <= row_of)
    half = drafts // 2
    t_half = lax.broadcasted_iota(jnp.int32, (1, half, 1), 1)
    head_of = lax.broadcasted_iota(jnp.int32, (MOVE * drafts, heads), 1)
    out_gain = og_ref[...].astype(F32)

    def tile(i, _):
        at = pl.ds(pl.multiple_of(i * width, width), width)
        acts = []
        for c in range(3):
            proj = jnp.dot(normed[...], wq[c, :, at], preferred_element_type=F32)
            ext[c, :, pl.ds(8, drafts), at] = (
                proj.astype(BF16).astype(F32).reshape(reqs, drafts, width)
            )
            taps = cw_ref[c, :, at].astype(F32)
            total = jnp.zeros((reqs, drafts, width), F32)
            for o in range(CONV):
                tap = taps[o : o + 1]
                total = total + ext[c, :, pl.ds(EXT0 + o, drafts), at] * tap
            acts.append(total * jax.nn.sigmoid(total))
        for g in range(group):
            h = i * group + g
            mine = slice(g * DK, (g + 1) * DK)
            queries[h] = (unit(acts[0][:, :, mine]) * DK ** (-0.5)).astype(BF16)
            keys[h] = unit(acts[1][:, :, mine])
            values[h] = acts[2][:, :, mine]
        return 0

    for i in range(tiles):
        w_copy(i).wait()
    lax.fori_loop(0, tiles, tile, 0, unroll=True)
    st_copy.wait()

    def delta(side):
        mine = pl.ds(side * MOVE, MOVE)
        kept_here = kept[side * MOVE : (side + 1) * MOVE]

        def heads_of(i, _):
            at = pl.ds(i * group, group)
            q = queries[at, mine].reshape(many, drafts, DK)
            k = keys[at, mine].reshape(many, drafts, DK)
            v = values[at, mine].reshape(many, drafts, DK)
            rate = []
            for g in range(group):
                rates = beta[pl.ds(side * MOVE * drafts, MOVE * drafts), :]
                rate.append(
                    jnp.sum(
                        jnp.where(head_of == i * group + g, rates, 0.0), axis=-1, keepdims=True
                    ).reshape(MOVE, drafts, 1)
                )
            rate = jnp.concatenate(rate, axis=0)
            kh, kl = split(k)
            stacked = jnp.concatenate([kh, kl, q], axis=1)
            recalled = []
            seen = []
            for g in range(group):
                for r in range(MOVE):
                    state = st[slot_at[side * MOVE + r], i * group + g]
                    got = jnp.dot(stacked[g * MOVE + r], state, preferred_element_type=F32)
                    recalled.append(got[:drafts] + got[drafts : 2 * drafts])
                    seen.append(got[2 * drafts :])
            u = rate * (v - jnp.stack(recalled))
            k0, k1 = k[:, :half], k[:, half:]
            rate0, rate1 = rate[:, :half], rate[:, half:]
            u0, u1 = u[:, :half], u[:, half:]
            for s in range(drafts - 1):
                if s < half:
                    key_s, u_s = k0[:, s : s + 1], u0[:, s : s + 1]
                else:
                    key_s, u_s = k1[:, s - half : s - half + 1], u1[:, s - half : s - half + 1]
                if s < half - 1:
                    near = jnp.sum(k0 * key_s, axis=-1, keepdims=True) * rate0
                    u0 = u0 - jnp.where(t_half > s, near, 0.0) * u_s
                near = jnp.sum(k1 * key_s, axis=-1, keepdims=True) * rate1
                if s >= half:
                    near = jnp.where(t_half + half > s, near, 0.0)
                u1 = u1 - near * u_s
            u = jnp.concatenate([u0, u1], axis=1)
            near = lax.dot_general(
                q.reshape(block, DK),
                kh.reshape(block, DK),
                (((1,), (1,)), ((), ())),
                preferred_element_type=F32,
            )
            near = jnp.where(causal, near, 0.0).astype(BF16)
            o = jnp.stack(seen).reshape(block, DK) + jnp.dot(
                near, u.astype(BF16).reshape(block, DK), preferred_element_type=F32
            )
            scale = lax.rsqrt(jnp.mean(o * o, axis=-1, keepdims=True) + 1e-06)
            o = (o * scale * out_gain).astype(BF16)
            rows_here = MOVE * drafts
            for g in range(group):
                columns = pl.ds(pl.multiple_of((i * group + g) * DK, DK), DK)
                on[pl.ds(side * rows_here, rows_here), columns] = o[
                    g * rows_here : (g + 1) * rows_here
                ]
            u = u.reshape(group, MOVE, drafts, DK) * kept_here[None]
            mh, ml = split(u.reshape(many, drafts, DK))
            shape = (group, MOVE, 3 * drafts, DK)
            kc[at, mine] = jnp.concatenate([kh, kl, kh], axis=1).reshape(shape)
            uc[at, mine] = jnp.concatenate([mh, mh, ml], axis=1).reshape(shape)
            return 0

        return heads_of

    def project(side):
        sums = []
        lines = pl.ds(side * MOVE * drafts, MOVE * drafts)
        for j in list(range(1, n_tp)) + [0]:
            to = lax.rem(mt + j, n_tp)
            at = pl.ds(pl.multiple_of(to * cols, cols), cols)
            part[side, j] = jnp.dot(
                on[lines, :], wo[:, at], preferred_element_type=F32
            ).astype(BF16)
            if j:
                copy = pltpu.make_async_remote_copy(
                    src_ref=part.at[side, j],
                    dst_ref=part_in.at[side, j],
                    send_sem=rs_send.at[side, j],
                    recv_sem=rs_recv.at[side, j],
                    device_id={"tp": to},
                    device_id_type=MESH,
                )
                copy.start()
                sums.append(copy)
        return sums

    def finish(side, sums):
        for copy in sums:
            copy.wait()
        total = part[side, 0].astype(F32)
        for j in range(1, n_tp):
            total = total + part_in[side, j].astype(F32)
        mine = pl.ds(side * MOVE, MOVE)
        columns = pl.ds(pl.multiple_of(mt * cols, cols), cols)
        total = xs[mine, :, columns].astype(F32) + total.reshape(MOVE, drafts, cols)
        live_here = live[side * MOVE : (side + 1) * MOVE]
        rows_done = jnp.where(live_here > 0, total, 0.0).astype(BF16)
        done[mine] = rows_done
        back[mine] = rows_done

    lax.fori_loop(0, tiles, delta(0), 0, unroll=True)
    wo_copy.wait()
    sums = project(0)
    second = delta(1)
    lax.fori_loop(0, 1, second, 0)
    finish(0, sums)
    returns = [to_left(done.at[pl.ds(0, MOVE)], back, ret_send, ret_recv)]
    lax.fori_loop(1, tiles, second, 0, unroll=True)
    sums = project(1)

    line_of = lax.broadcasted_iota(jnp.int32, (reqs, 8 + drafts, 1), 1)
    first = EXT0 + spread(keeps, (reqs, 8 + drafts, 1))

    def edges(c, _):
        for e in range(HIST):
            chosen = jnp.sum(jnp.where(line_of == first + e, ext[c], 0.0), axis=1)
            fconv_ref[e, c] = jnp.dot(
                to_slot, chosen.astype(BF16), preferred_element_type=F32
            ).astype(BF16)
        return 0

    lax.fori_loop(0, 3, edges, 0)
    finish(1, sums)
    returns.append(to_right(done.at[pl.ds(MOVE, MOVE)], back, ret_send, ret_recv))

    def page_copy(h):
        return pltpu.make_async_copy(pages_ref.at[:, h], pages_hbm.at[:, h], out_sem.at[h])

    def accept(h, _):
        for j in range(reqs):
            gained = lax.dot_general(
                kc[h, spot[j]], uc[h, spot[j]], (((0,), (0,)), ((), ())), preferred_element_type=F32
            )
            pages_ref[j, h] = (st[j, h].astype(F32) + gained).astype(BF16)
        page_copy(h).start()
        return 0

    def drain(h, _):
        page_copy(h).wait()
        return 0

    lax.fori_loop(0, heads, accept, 0)
    for copy in returns:
        copy.wait()
    for i in range(reqs):
        mixed_ref[i] = back[homes[i]]
    lax.fori_loop(0, heads, drain, 0)


def hand_out(mixed_in, fconv_in, pages_in, mixed_out, fconv_out, pages_out, *scratch):
    mixed, fconv, pages, in_sem, out_sem = scratch
    reqs = pages_in.shape[0]
    routes = [(pages_in.at[j], pages.at[j], pages_out.at[j]) for j in range(reqs)]
    routes += [(mixed_in, mixed, mixed_out), (fconv_in, fconv, fconv_out)]
    reads = [pltpu.make_async_copy(r[0], r[1], in_sem.at[i]) for i, r in enumerate(routes)]
    writes = [pltpu.make_async_copy(r[1], r[2], out_sem.at[i]) for i, r in enumerate(routes)]
    for read in reads:
        read.start()
    for read, write in zip(reads, writes):
        read.wait()
        write.start()
    for write in writes:
        write.wait()


def on_device(
    n_seq,
    n_tp,
    tokens,
    gain_in,
    w_qkv,
    w_beta,
    conv_weight,
    out_gain,
    w_out,
    state_pages,
    conv_pages,
    page_order,
    draft_lengths,
    accepted,
):
    reqs, drafts, cols = tokens.shape
    rows = reqs * drafts
    depth = w_qkv.shape[1]
    heads = state_pages.shape[1]
    hidden = heads * DK
    vmem = pl.BlockSpec(memory_space=pltpu.VMEM)
    hbm = pl.BlockSpec(memory_space=pltpu.HBM)
    dma = pltpu.SemaphoreType.DMA
    results = pl.pallas_call(
        functools.partial(kernel, n_seq, n_tp),
        out_shape=(
            jax.ShapeDtypeStruct(tokens.shape, BF16),
            jax.ShapeDtypeStruct((HIST, 3, reqs, hidden), BF16),
            jax.ShapeDtypeStruct(state_pages.shape, BF16),
        ),
        in_specs=[hbm] * 12,
        out_specs=(vmem, vmem, hbm),
        scratch_shapes=[
            pltpu.SMEM(page_order.shape, jnp.int32),
            pltpu.SMEM(draft_lengths.shape, jnp.int32),
            pltpu.SMEM(accepted.shape, jnp.int32),
            pltpu.VMEM(tokens.shape, BF16),
            pltpu.VMEM(gain_in.shape, BF16),
            pltpu.VMEM((heads, depth), BF16),
            pltpu.VMEM((3, CONV, hidden), BF16),
            pltpu.VMEM((1, DK), BF16),
            pltpu.VMEM((HIST, 3, reqs, hidden), BF16),
            pltpu.VMEM(w_qkv.shape, BF16),
            pltpu.VMEM(w_out.shape, BF16),
            pltpu.VMEM(state_pages.shape, BF16),
            pltpu.VMEM((n_tp, reqs + 2 * MOVE, drafts, cols), BF16),
            pltpu.VMEM((MOVE, drafts, cols), BF16),
            pltpu.VMEM((MOVE, drafts, cols), BF16),
            pltpu.VMEM((reqs, drafts, depth), BF16),
            pltpu.VMEM((rows, depth), BF16),
            pltpu.VMEM((3, reqs, 8 + drafts, hidden), F32),
            pltpu.VMEM((heads, reqs, drafts, DK), BF16),
            pltpu.VMEM((heads, reqs, drafts, DK), F32),
            pltpu.VMEM((heads, reqs, drafts, DK), F32),
            pltpu.VMEM((rows, heads), F32),
            pltpu.VMEM((rows, hidden), BF16),
            pltpu.VMEM((heads, reqs, 3 * drafts, DK), BF16),
            pltpu.VMEM((heads, reqs, 3 * drafts, DK), BF16),
            pltpu.VMEM((2, n_tp, MOVE * drafts, cols), BF16),
            pltpu.VMEM((2, n_tp, MOVE * drafts, cols), BF16),
            pltpu.VMEM(tokens.shape, BF16),
            pltpu.VMEM((reqs + 2 * MOVE, drafts, cols), BF16),
            pltpu.VMEM(state_pages.shape, BF16),
            dma((9,)),
            dma((heads,)),
            dma((heads,)),
            dma,
            dma,
            dma((2,)),
            dma((2,)),
            dma((2, n_tp)),
            dma((2, n_tp)),
            dma((2, n_tp)),
            dma((2, n_tp)),
            dma((2,)),
            dma((2,)),
        ],
        compiler_params=pltpu.CompilerParams(
            collective_id=0, has_side_effects=True, vmem_limit_bytes=60 * 1024 * 1024
        ),
    )(
        page_order,
        draft_lengths,
        accepted,
        tokens,
        gain_in,
        w_beta.T,
        jnp.transpose(conv_weight, (1, 0, 2)),
        out_gain.reshape(1, -1),
        jnp.transpose(conv_pages, (1, 2, 0, 3)),
        w_qkv,
        w_out,
        state_pages,
    )
    mixed, final_conv, pages = pl.pallas_call(
        hand_out,
        out_shape=tuple(jax.ShapeDtypeStruct(a.shape, a.dtype) for a in results),
        in_specs=[hbm] * 3,
        out_specs=(hbm,) * 3,
        scratch_shapes=[pltpu.VMEM(a.shape, a.dtype) for a in results]
        + [dma((reqs + 2,)), dma((reqs + 2,))],
        compiler_params=pltpu.CompilerParams(vmem_limit_bytes=60 * 1024 * 1024),
    )(*results)
    return mixed, pages, jnp.transpose(final_conv, (2, 0, 1, 3))


def solution(mesh):
    return jax.shard_map(
        functools.partial(on_device, mesh.shape["seq"], mesh.shape["tp"]),
        mesh=mesh,
        in_specs=(
            P("seq", None, "tp"),
            P(),
            P(None, None, "tp"),
            P(None, "tp"),
            P(None, None, "tp"),
            P(),
            P("tp", None),
            P("seq", "tp", None, None),
            P("seq", None, None, "tp"),
            P(),
            P(),
            P(),
        ),
        out_specs=(P("seq", None, "tp"), P("seq", "tp", None, None), P("seq", None, None, "tp")),
        check_vma=False,
    )
```

```python
import functools

import jax
import jax.numpy as jnp
from jax import lax
from jax.experimental import pallas as pl
from jax.experimental.pallas import tpu as pltpu
from jax.sharding import PartitionSpec as P

DK = 128
CONV = 4
MOVE = 4
HIST = CONV - 1
EXT0 = 8 - HIST
F32 = jnp.float32
BF16 = jnp.bfloat16
MESH = pl.DeviceIdType.MESH


def split(wide):
    high = wide.astype(BF16)
    return high, (wide - high.astype(F32)).astype(BF16)


def unit(values):
    return values * lax.rsqrt(jnp.sum(values * values, axis=-1, keepdims=True) + 1e-06)


def matches(po_ref, device, home, reqs):
    found = []
    count = jnp.int32(0)
    for j in range(reqs):
        request = po_ref[device * reqs + j]
        hit = (request >= home * reqs) & (request < home * reqs + reqs)
        found.append((request, hit, count))
        count = count + hit.astype(jnp.int32)
    return found


def pick_rank(found, rank, values):
    total = jnp.int32(0)
    for (_, hit, place), value in zip(found, values):
        total = total + jnp.where(hit & (place == rank), value, 0)
    return jnp.clip(total, 0, len(values) - 1)


def kernel(
    n_seq,
    n_tp,
    po_hbm,
    len_hbm,
    acc_hbm,
    tok_hbm,
    gain_hbm,
    wb_hbm,
    cw_hbm,
    og_hbm,
    conv_hbm,
    wqkv_hbm,
    wout_hbm,
    state_hbm,
    mixed_ref,
    fconv_ref,
    pages_hbm,
    po_ref,
    len_ref,
    acc_ref,
    tok_ref,
    gain_ref,
    wb_ref,
    cw_ref,
    og_ref,
    conv_ref,
    wq,
    wo,
    st,
    pool,
    send_l,
    send_r,
    xs,
    normed,
    ext,
    queries,
    keys,
    values,
    beta,
    on,
    kc,
    uc,
    part,
    part_in,
    done,
    back,
    pages_ref,
    in_sem,
    out_sem,
    w_sem,
    wo_sem,
    st_sem,
    mig_send,
    mig_recv,
    tp_send,
    tp_recv,
    rs_send,
    rs_recv,
    ret_send,
    ret_recv,
):
    reqs, drafts, cols = tok_ref.shape
    rows = reqs * drafts
    heads = state_hbm.shape[1]
    hidden = heads * DK
    group = 2 if heads % 2 == 0 else 1
    width = group * DK
    tiles = heads // group
    me = lax.axis_index("seq")
    mt = lax.axis_index("tp")
    left = lax.rem(me + n_seq - 1, n_seq)
    right = lax.rem(me + 1, n_seq)

    def w_copy(i):
        at = pl.ds(pl.multiple_of(i * width, width), width)
        return pltpu.make_async_copy(wqkv_hbm.at[:, :, at], wq.at[:, :, at], w_sem.at[i])

    st_copy = pltpu.make_async_copy(state_hbm, st, st_sem)
    wo_copy = pltpu.make_async_copy(wout_hbm, wo, wo_sem)
    small = []
    pairs = (
        (po_hbm, po_ref),
        (len_hbm, len_ref),
        (acc_hbm, acc_ref),
        (tok_hbm, tok_ref),
        (conv_hbm, conv_ref),
        (gain_hbm, gain_ref),
        (wb_hbm, wb_ref),
        (cw_hbm, cw_ref),
        (og_hbm, og_ref),
    )
    for i, (src, dst) in enumerate(pairs):
        small.append(pltpu.make_async_copy(src, dst, in_sem.at[i]))
        small[i].start()
    w_copy(0).start()
    st_copy.start()
    for i in range(1, tiles):
        w_copy(i).start()
    wo_copy.start()

    barrier = pltpu.get_barrier_semaphore()
    for other in (left, right):
        pl.semaphore_signal(barrier, inc=1, device_id={"seq": other}, device_id_type=MESH)
    for j in range(1, n_tp):
        pl.semaphore_signal(
            barrier, inc=1, device_id={"tp": lax.rem(mt + j, n_tp)}, device_id_type=MESH
        )

    for copy in small[:4]:
        copy.wait()
    own = matches(po_ref, me, me, reqs)
    from_l = matches(po_ref, me, left, reqs)
    from_r = matches(po_ref, me, right, reqs)
    at_l = matches(po_ref, left, me, reqs)
    at_r = matches(po_ref, right, me, reqs)
    base = me * reqs
    for k in range(MOVE):
        send_l[k] = tok_ref[pick_rank(at_l, k, [f[0] - base for f in at_l])]
        send_r[k] = tok_ref[pick_rank(at_r, k, [f[0] - base for f in at_r])]
    pl.semaphore_wait(barrier, 2 + n_tp - 1)

    def to_right(src, dst, send_sem, recv_sem):
        copy = pltpu.make_async_remote_copy(
            src_ref=src,
            dst_ref=dst.at[pl.ds(reqs, MOVE)],
            send_sem=send_sem.at[0],
            recv_sem=recv_sem.at[0],
            device_id={"seq": right},
            device_id_type=MESH,
        )
        copy.start()
        return copy

    def to_left(src, dst, send_sem, recv_sem):
        copy = pltpu.make_async_remote_copy(
            src_ref=src,
            dst_ref=dst.at[pl.ds(reqs + MOVE, MOVE)],
            send_sem=send_sem.at[1],
            recv_sem=recv_sem.at[1],
            device_id={"seq": left},
            device_id_type=MESH,
        )
        copy.start()
        return copy

    moves = [
        to_right(send_r, pool.at[mt], mig_send, mig_recv),
        to_left(send_l, pool.at[mt], mig_send, mig_recv),
    ]

    def to_peers(src, dst, stage):
        copies = []
        for j in range(1, n_tp):
            copy = pltpu.make_async_remote_copy(
                src_ref=src,
                dst_ref=dst,
                send_sem=tp_send.at[stage, j],
                recv_sem=tp_recv.at[stage, j],
                device_id={"tp": lax.rem(mt + j, n_tp)},
                device_id_type=MESH,
            )
            copy.start()
            copies.append(copy)
        return copies

    gathers = to_peers(tok_ref, pool.at[mt, pl.ds(0, reqs)], 0)
    pool[mt, pl.ds(0, reqs)] = tok_ref[...]

    count_l = jnp.int32(0)
    count_r = jnp.int32(0)
    for j in range(reqs):
        count_l = count_l + from_l[j][1].astype(jnp.int32)
        count_r = count_r + from_r[j][1].astype(jnp.int32)
    spot = []
    places = []
    for j in range(reqs):
        rank = own[j][2]
        room = MOVE - count_l
        here = jnp.where(rank < room, count_l + rank, MOVE + count_r + rank - room)
        other = jnp.where(from_l[j][1], from_l[j][2], MOVE + from_r[j][2])
        spot.append(jnp.clip(jnp.where(own[j][1], here, other), 0, reqs - 1))
        place = jnp.where(from_l[j][1], reqs + from_l[j][2], reqs + MOVE + from_r[j][2])
        place = jnp.where(own[j][1], own[j][0] - base, place)
        places.append(jnp.clip(place, 0, reqs + 2 * MOVE - 1))
    slot_at = []
    place_at = []
    lengths = []
    keeps = []
    for p in range(reqs):
        slot = jnp.int32(0)
        place = jnp.int32(0)
        request = jnp.int32(0)
        for j in range(reqs):
            hit = spot[j] == p
            slot = jnp.where(hit, j, slot)
            place = jnp.where(hit, places[j], place)
            request = jnp.where(hit, own[j][0], request)
        slot_at.append(slot)
        place_at.append(place)
        lengths.append(len_ref[request])
        keeps.append(jnp.minimum(acc_ref[request], lengths[p]))
    homes = []
    for i in range(reqs):
        place = jnp.int32(0)
        for j in range(reqs):
            place = jnp.where(own[j][0] == base + i, spot[j], place)
            place = jnp.where(at_l[j][0] == base + i, reqs + at_l[j][2], place)
            place = jnp.where(at_r[j][0] == base + i, reqs + MOVE + at_r[j][2], place)
        homes.append(jnp.clip(place, 0, reqs + 2 * MOVE - 1))

    def spread(numbers, shape):
        index = lax.broadcasted_iota(jnp.int32, shape, 0)
        out = jnp.zeros(shape, jnp.int32)
        for p in range(reqs):
            out = jnp.where(index == p, numbers[p], out)
        return out

    step_of = lax.broadcasted_iota(jnp.int32, (reqs, drafts, 1), 1)
    live = (step_of < spread(lengths, (reqs, drafts, 1))).astype(F32)
    kept = (step_of < spread(keeps, (reqs, drafts, 1))).astype(F32)
    lane_of = lax.broadcasted_iota(jnp.int32, (reqs, reqs), 1)
    to_spot = (lane_of == spread(slot_at, (reqs, reqs))).astype(F32).astype(BF16)
    to_slot = (lane_of == spread(spot, (reqs, reqs))).astype(F32).astype(BF16)
    for copy in small[4:]:
        copy.wait()
    for e in range(HIST):
        for c in range(3):
            ext[c, :, EXT0 + e, :] = jnp.dot(
                to_spot, conv_ref[e, c], preferred_element_type=F32
            )

    for copy in moves:
        copy.wait()
    gathers += to_peers(
        pool.at[mt, pl.ds(reqs, 2 * MOVE)], pool.at[mt, pl.ds(reqs, 2 * MOVE)], 1
    )
    for copy in gathers:
        copy.wait()

    gain = gain_ref[...].astype(F32).reshape(1, -1)
    for j in range(reqs):
        for c in range(n_tp):
            xs[j, :, pl.ds(c * cols, cols)] = pool[c, place_at[j]]
        wide = xs[j].astype(F32)
        scale = lax.rsqrt(jnp.mean(wide * wide, axis=-1, keepdims=True) + 1e-06)
        normed[pl.ds(j * drafts, drafts), :] = (wide * scale * gain).astype(BF16)
    rates = jax.nn.sigmoid(
        lax.dot_general(
            normed[...], wb_ref[...], (((1,), (1,)), ((), ())), preferred_element_type=F32
        )
    )
    beta[...] = rates * live.reshape(rows, 1)

    many = group * MOVE
    block = many * drafts
    row_of = lax.broadcasted_iota(jnp.int32, (block, block), 0)
    col_of = lax.broadcasted_iota(jnp.int32, (block, block), 1)
    causal = (row_of // drafts == col_of // drafts) & (col_of <= row_of)
    half = drafts // 2
    t_half = lax.broadcasted_iota(jnp.int32, (1, half, 1), 1)
    head_of = lax.broadcasted_iota(jnp.int32, (MOVE * drafts, heads), 1)
    out_gain = og_ref[...].astype(F32)

    def tile(i, _):
        at = pl.ds(pl.multiple_of(i * width, width), width)
        acts = []
        for c in range(3):
            proj = jnp.dot(normed[...], wq[c, :, at], preferred_element_type=F32)
            ext[c, :, pl.ds(8, drafts), at] = (
                proj.astype(BF16).astype(F32).reshape(reqs, drafts, width)
            )
            taps = cw_ref[c, :, at].astype(F32)
            total = jnp.zeros((reqs, drafts, width), F32)
            for o in range(CONV):
                tap = taps[o : o + 1]
                total = total + ext[c, :, pl.ds(EXT0 + o, drafts), at] * tap
            acts.append(total * jax.nn.sigmoid(total))
        for g in range(group):
            h = i * group + g
            mine = slice(g * DK, (g + 1) * DK)
            queries[h] = (unit(acts[0][:, :, mine]) * DK ** (-0.5)).astype(BF16)
            keys[h] = unit(acts[1][:, :, mine])
            values[h] = acts[2][:, :, mine]
        return 0

    for i in range(tiles):
        w_copy(i).wait()
    lax.fori_loop(0, tiles, tile, 0, unroll=True)
    st_copy.wait()

    def delta(side):
        mine = pl.ds(side * MOVE, MOVE)
        kept_here = kept[side * MOVE : (side + 1) * MOVE]

        def heads_of(i, _):
            at = pl.ds(i * group, group)
            q = queries[at, mine].reshape(many, drafts, DK)
            k = keys[at, mine].reshape(many, drafts, DK)
            v = values[at, mine].reshape(many, drafts, DK)
            rate = []
            for g in range(group):
                rates = beta[pl.ds(side * MOVE * drafts, MOVE * drafts), :]
                rate.append(
                    jnp.sum(
                        jnp.where(head_of == i * group + g, rates, 0.0), axis=-1, keepdims=True
                    ).reshape(MOVE, drafts, 1)
                )
            rate = jnp.concatenate(rate, axis=0)
            kh, kl = split(k)
            stacked = jnp.concatenate([kh, kl, q], axis=1)
            recalled = []
            seen = []
            for g in range(group):
                for r in range(MOVE):
                    state = st[slot_at[side * MOVE + r], i * group + g]
                    got = jnp.dot(stacked[g * MOVE + r], state, preferred_element_type=F32)
                    recalled.append(got[:drafts] + got[drafts : 2 * drafts])
                    seen.append(got[2 * drafts :])
            u = rate * (v - jnp.stack(recalled))
            k0, k1 = k[:, :half], k[:, half:]
            rate0, rate1 = rate[:, :half], rate[:, half:]
            u0, u1 = u[:, :half], u[:, half:]
            for s in range(drafts - 1):
                if s < half:
                    key_s, u_s = k0[:, s : s + 1], u0[:, s : s + 1]
                else:
                    key_s, u_s = k1[:, s - half : s - half + 1], u1[:, s - half : s - half + 1]
                if s < half - 1:
                    near = jnp.sum(k0 * key_s, axis=-1, keepdims=True) * rate0
                    u0 = u0 - jnp.where(t_half > s, near, 0.0) * u_s
                near = jnp.sum(k1 * key_s, axis=-1, keepdims=True) * rate1
                if s >= half:
                    near = jnp.where(t_half + half > s, near, 0.0)
                u1 = u1 - near * u_s
            u = jnp.concatenate([u0, u1], axis=1)
            near = lax.dot_general(
                q.reshape(block, DK),
                kh.reshape(block, DK),
                (((1,), (1,)), ((), ())),
                preferred_element_type=F32,
            )
            near = jnp.where(causal, near, 0.0).astype(BF16)
            o = jnp.stack(seen).reshape(block, DK) + jnp.dot(
                near, u.astype(BF16).reshape(block, DK), preferred_element_type=F32
            )
            scale = lax.rsqrt(jnp.mean(o * o, axis=-1, keepdims=True) + 1e-06)
            o = (o * scale * out_gain).astype(BF16)
            rows_here = MOVE * drafts
            for g in range(group):
                columns = pl.ds(pl.multiple_of((i * group + g) * DK, DK), DK)
                on[pl.ds(side * rows_here, rows_here), columns] = o[
                    g * rows_here : (g + 1) * rows_here
                ]
            u = u.reshape(group, MOVE, drafts, DK) * kept_here[None]
            mh, ml = split(u.reshape(many, drafts, DK))
            shape = (group, MOVE, 3 * drafts, DK)
            kc[at, mine] = jnp.concatenate([kh, kl, kh], axis=1).reshape(shape)
            uc[at, mine] = jnp.concatenate([mh, mh, ml], axis=1).reshape(shape)
            return 0

        return heads_of

    def project(side):
        sums = []
        lines = pl.ds(side * MOVE * drafts, MOVE * drafts)
        for j in list(range(1, n_tp)) + [0]:
            to = lax.rem(mt + j, n_tp)
            at = pl.ds(pl.multiple_of(to * cols, cols), cols)
            part[side, j] = jnp.dot(
                on[lines, :], wo[:, at], preferred_element_type=F32
            ).astype(BF16)
            if j:
                copy = pltpu.make_async_remote_copy(
                    src_ref=part.at[side, j],
                    dst_ref=part_in.at[side, j],
                    send_sem=rs_send.at[side, j],
                    recv_sem=rs_recv.at[side, j],
                    device_id={"tp": to},
                    device_id_type=MESH,
                )
                copy.start()
                sums.append(copy)
        return sums

    def finish(side, sums):
        for copy in sums:
            copy.wait()
        total = part[side, 0].astype(F32)
        for j in range(1, n_tp):
            total = total + part_in[side, j].astype(F32)
        mine = pl.ds(side * MOVE, MOVE)
        columns = pl.ds(pl.multiple_of(mt * cols, cols), cols)
        total = xs[mine, :, columns].astype(F32) + total.reshape(MOVE, drafts, cols)
        live_here = live[side * MOVE : (side + 1) * MOVE]
        rows_done = jnp.where(live_here > 0, total, 0.0).astype(BF16)
        done[mine] = rows_done
        back[mine] = rows_done

    lax.fori_loop(0, tiles, delta(0), 0, unroll=True)
    wo_copy.wait()
    sums = project(0)
    second = delta(1)
    lax.fori_loop(0, 1, second, 0)
    finish(0, sums)
    returns = [to_left(done.at[pl.ds(0, MOVE)], back, ret_send, ret_recv)]
    lax.fori_loop(1, tiles, second, 0, unroll=True)
    sums = project(1)

    line_of = lax.broadcasted_iota(jnp.int32, (reqs, 8 + drafts, 1), 1)
    first = EXT0 + spread(keeps, (reqs, 8 + drafts, 1))

    def edges(c, _):
        for e in range(HIST):
            chosen = jnp.sum(jnp.where(line_of == first + e, ext[c], 0.0), axis=1)
            fconv_ref[e, c] = jnp.dot(
                to_slot, chosen.astype(BF16), preferred_element_type=F32
            ).astype(BF16)
        return 0

    finish(1, sums)
    returns.append(to_right(done.at[pl.ds(MOVE, MOVE)], back, ret_send, ret_recv))

    def page_copy(h):
        return pltpu.make_async_copy(pages_ref.at[:, h], pages_hbm.at[:, h], out_sem.at[h])

    def accept(h, _):
        for j in range(reqs):
            gained = lax.dot_general(
                kc[h, spot[j]], uc[h, spot[j]], (((0,), (0,)), ((), ())), preferred_element_type=F32
            )
            pages_ref[j, h] = (st[j, h].astype(F32) + gained).astype(BF16)
        page_copy(h).start()
        return 0

    def drain(h, _):
        page_copy(h).wait()
        return 0

    lax.fori_loop(0, heads, accept, 0)
    lax.fori_loop(0, 3, edges, 0)
    for copy in returns:
        copy.wait()
    for i in range(reqs):
        mixed_ref[i] = back[homes[i]]
    lax.fori_loop(0, heads, drain, 0)


def hand_out(mixed_in, fconv_in, pages_in, mixed_out, fconv_out, pages_out, *scratch):
    mixed, fconv, pages, in_sem, out_sem = scratch
    reqs = pages_in.shape[0]
    routes = [(pages_in.at[j], pages.at[j], pages_out.at[j]) for j in range(reqs)]
    routes += [(mixed_in, mixed, mixed_out), (fconv_in, fconv, fconv_out)]
    reads = [pltpu.make_async_copy(r[0], r[1], in_sem.at[i]) for i, r in enumerate(routes)]
    writes = [pltpu.make_async_copy(r[1], r[2], out_sem.at[i]) for i, r in enumerate(routes)]
    for read in reads:
        read.start()
    for read, write in zip(reads, writes):
        read.wait()
        write.start()
    for write in writes:
        write.wait()


def on_device(
    n_seq,
    n_tp,
    tokens,
    gain_in,
    w_qkv,
    w_beta,
    conv_weight,
    out_gain,
    w_out,
    state_pages,
    conv_pages,
    page_order,
    draft_lengths,
    accepted,
):
    reqs, drafts, cols = tokens.shape
    rows = reqs * drafts
    depth = w_qkv.shape[1]
    heads = state_pages.shape[1]
    hidden = heads * DK
    vmem = pl.BlockSpec(memory_space=pltpu.VMEM)
    hbm = pl.BlockSpec(memory_space=pltpu.HBM)
    dma = pltpu.SemaphoreType.DMA
    results = pl.pallas_call(
        functools.partial(kernel, n_seq, n_tp),
        out_shape=(
            jax.ShapeDtypeStruct(tokens.shape, BF16),
            jax.ShapeDtypeStruct((HIST, 3, reqs, hidden), BF16),
            jax.ShapeDtypeStruct(state_pages.shape, BF16),
        ),
        in_specs=[hbm] * 12,
        out_specs=(vmem, vmem, hbm),
        scratch_shapes=[
            pltpu.SMEM(page_order.shape, jnp.int32),
            pltpu.SMEM(draft_lengths.shape, jnp.int32),
            pltpu.SMEM(accepted.shape, jnp.int32),
            pltpu.VMEM(tokens.shape, BF16),
            pltpu.VMEM(gain_in.shape, BF16),
            pltpu.VMEM((heads, depth), BF16),
            pltpu.VMEM((3, CONV, hidden), BF16),
            pltpu.VMEM((1, DK), BF16),
            pltpu.VMEM((HIST, 3, reqs, hidden), BF16),
            pltpu.VMEM(w_qkv.shape, BF16),
            pltpu.VMEM(w_out.shape, BF16),
            pltpu.VMEM(state_pages.shape, BF16),
            pltpu.VMEM((n_tp, reqs + 2 * MOVE, drafts, cols), BF16),
            pltpu.VMEM((MOVE, drafts, cols), BF16),
            pltpu.VMEM((MOVE, drafts, cols), BF16),
            pltpu.VMEM((reqs, drafts, depth), BF16),
            pltpu.VMEM((rows, depth), BF16),
            pltpu.VMEM((3, reqs, 8 + drafts, hidden), F32),
            pltpu.VMEM((heads, reqs, drafts, DK), BF16),
            pltpu.VMEM((heads, reqs, drafts, DK), F32),
            pltpu.VMEM((heads, reqs, drafts, DK), F32),
            pltpu.VMEM((rows, heads), F32),
            pltpu.VMEM((rows, hidden), BF16),
            pltpu.VMEM((heads, reqs, 3 * drafts, DK), BF16),
            pltpu.VMEM((heads, reqs, 3 * drafts, DK), BF16),
            pltpu.VMEM((2, n_tp, MOVE * drafts, cols), BF16),
            pltpu.VMEM((2, n_tp, MOVE * drafts, cols), BF16),
            pltpu.VMEM(tokens.shape, BF16),
            pltpu.VMEM((reqs + 2 * MOVE, drafts, cols), BF16),
            pltpu.VMEM(state_pages.shape, BF16),
            dma((9,)),
            dma((heads,)),
            dma((heads,)),
            dma,
            dma,
            dma((2,)),
            dma((2,)),
            dma((2, n_tp)),
            dma((2, n_tp)),
            dma((2, n_tp)),
            dma((2, n_tp)),
            dma((2,)),
            dma((2,)),
        ],
        compiler_params=pltpu.CompilerParams(
            collective_id=0, has_side_effects=True, vmem_limit_bytes=60 * 1024 * 1024
        ),
    )(
        page_order,
        draft_lengths,
        accepted,
        tokens,
        gain_in,
        w_beta.T,
        jnp.transpose(conv_weight, (1, 0, 2)),
        out_gain.reshape(1, -1),
        jnp.transpose(conv_pages, (1, 2, 0, 3)),
        w_qkv,
        w_out,
        state_pages,
    )
    mixed, final_conv, pages = pl.pallas_call(
        hand_out,
        out_shape=tuple(jax.ShapeDtypeStruct(a.shape, a.dtype) for a in results),
        in_specs=[hbm] * 3,
        out_specs=(hbm,) * 3,
        scratch_shapes=[pltpu.VMEM(a.shape, a.dtype) for a in results]
        + [dma((reqs + 2,)), dma((reqs + 2,))],
        compiler_params=pltpu.CompilerParams(vmem_limit_bytes=60 * 1024 * 1024),
    )(*results)
    return mixed, pages, jnp.transpose(final_conv, (2, 0, 1, 3))


def solution(mesh):
    return jax.shard_map(
        functools.partial(on_device, mesh.shape["seq"], mesh.shape["tp"]),
        mesh=mesh,
        in_specs=(
            P("seq", None, "tp"),
            P(),
            P(None, None, "tp"),
            P(None, "tp"),
            P(None, None, "tp"),
            P(),
            P("tp", None),
            P("seq", "tp", None, None),
            P("seq", None, None, "tp"),
            P(),
            P(),
            P(),
        ),
        out_specs=(P("seq", None, "tp"), P("seq", "tp", None, None), P("seq", None, None, "tp")),
        check_vma=False,
    )
```
